32 devices in a mesh: ma: 8 (over z, x), band: 4 (over y, core).
Axes of the slice: x: 2, y: 2, z: 4, core: 2. Of those that a mesh axis runs over, the one named last changes fastest.
Arguments:
- harmonics: bfloat16 [32, 8192, 256], P(('ma', 'band')), may hold values from -6 to 6
- legendre: bfloat16 [32, 2, 8192, 128], P(('ma', 'band')), may hold values from -0.005859375 to 0.005859375
- m_values: int32 [32], replicated, may hold values from 1 to 8191
- cycle_cell: int32 [4096], P(('ma', 'band')), may hold values from 0 to 31, as said below
- phi_cell: int32 [4096], P(('ma', 'band')), may hold values from 3 to 123
- offsets: float32 [2, 4096], P(None, ('ma', 'band')), may hold values from 0 to 1
Outputs:
- lensed: float32 [4096, 128], P(('ma', 'band'))
The draws below stay inside these ranges and needn't reach their ends.
Inputs may be any that keep to these rules, and one draw needn't show every extreme that they name: `cycle_cell`: Band-local cycle; every point held by device (ma, band) lies in latitude band `band`. For each device and each ma index q, at most 16 of its points have cycles q * 4 to q * 4 + 3, and in every band one q receives exactly 16 points from every device of the band.
All inputs are finite; a program needn't handle non-finite values.
Results may differ from the reference program's by a relative error of at most 0.0053.
Values may be sent and summed in bfloat16 or wider, within the bound.
A program may use at most 64 MiB of HBM per device.

```python
import jax
import jax.numpy as jnp
from jax import lax

L = 8192
NSIM = 64
NPHI = 128
PD = 128
RD = 4
OWNERS = 8
BANDS = 4
MTOT = 32
R = 128
RB = 32
CAP = 16
PTS = 4096


def draw_cycle_cell(key, part):
    blocks = OWNERS * BANDS
    hot_owner = jax.random.randint(jax.random.fold_in(key, 11), (BANDS,), 0, OWNERS)
    block_keys = jax.random.split(jax.random.fold_in(key, 12), blocks)

    def one_block(block_key, band_index):
        key_pick, key_order, key_cycle = jax.random.split(block_key, 3)
        picked = jax.random.permutation(key_pick, (OWNERS - 1) * CAP)[:PD - CAP] // CAP + 1
        steps_away = jnp.concatenate([jnp.zeros((CAP,), jnp.int32), picked.astype(jnp.int32)])
        steps_away = jax.random.permutation(key_order, steps_away)
        owner_index = (hot_owner[band_index] + steps_away) % OWNERS
        return owner_index * RD + jax.random.randint(key_cycle, (PD,), 0, RD)
    drawn = jax.vmap(one_block)(block_keys, jnp.arange(blocks) % BANDS)
    return drawn.reshape(-1).astype(jnp.int32)


def place_ends(values, own_key, low, largest):
    spot = [jax.random.randint(jax.random.fold_in(own_key, axis), (), 0, length) for axis, length in enumerate(values.shape)]
    longest = values.shape.index(max(values.shape))
    neighbour = spot[:longest] + [(spot[longest] + 1) % values.shape[longest]] + spot[longest + 1:]
    return values.at[tuple(spot)].set(low).at[tuple(neighbour)].set(largest)


def block_levels(rng, extent, pieces, smallest, largest):
    level, own = 1.0, jax.random.fold_in(rng, 6)
    for axis_at, blocks in pieces:
        heights = jnp.exp(jax.random.uniform(jax.random.fold_in(own, axis_at), (blocks,), jnp.float32, smallest / len(pieces), largest / len(pieces)))
        level = level * jnp.repeat(heights, extent[axis_at] // blocks).reshape([-1 if axis == axis_at else 1 for axis in range(len(extent))])
    return level


def gaussian(rng, shape, deviation, bound, cuts=(), kind=jnp.bfloat16):
    values = jax.random.normal(rng, shape, jnp.float32) * deviation
    if len(cuts) > 0:
        values = block_levels(rng, shape, cuts, -0.22, 0.18) * values
    return jnp.clip(values, min=-bound, max=bound).astype(kind)


def setup_inputs(seed: int = 0) -> dict:
    streams_of = jax.random.split(jax.random.key(seed), 7)
    harmonics = gaussian(streams_of[0], (MTOT, L, 4 * NSIM), 1.0, 6.0, ((0, 32),))
    legendre = gaussian(streams_of[1], (MTOT, 2, L, R), (4 * L * MTOT) ** -0.5, 0.005859375, ((0, 32),))
    m_values = place_ends(jax.random.randint(streams_of[2], (MTOT,), 1, L), jax.random.fold_in(streams_of[2], 1), 1, L - 1).astype(jnp.int32)
    cycle_cell = draw_cycle_cell(jax.random.fold_in(streams_of[6], 71), 0)
    phi_cell = place_ends(jax.random.randint(streams_of[4], (PTS,), 3, NPHI - 4), jax.random.fold_in(streams_of[4], 1), 3, (NPHI - 4) - 1).astype(jnp.int32)
    offsets = jnp.clip(1.0 * jax.random.uniform(streams_of[5], (2, PTS), jnp.float32) ** block_levels(streams_of[5], (2, PTS), ((1, 32),), -0.2, 0.2), 0.0, 1.0)
    return dict(harmonics=harmonics, legendre=legendre, m_values=m_values, cycle_cell=cycle_cell, phi_cell=phi_cell, offsets=offsets)


def kernel_taps(shifts):
    return jnp.sinc(shifts) * jnp.sinc(shifts / 4.0)


def tap_weights(offset_pairs):
    tap_shift = jnp.arange(8).astype(jnp.float32) - 3.0
    across = kernel_taps(tap_shift[None, :] - offset_pairs[:, 0:1])
    beside_all = kernel_taps(tap_shift[None, :] - offset_pairs[:, 1:2])
    return (across[:, :, None] * beside_all[:, None, :]).astype(jnp.bfloat16)


def combine_parts(plus_part, minus_part):
    q_real = -(plus_part[:, 0, 0] - minus_part[:, 1, 1])
    q_imag = -(plus_part[:, 0, 1] + minus_part[:, 1, 0])
    u_real = -(plus_part[:, 1, 0] + minus_part[:, 0, 1])
    u_imag = -(plus_part[:, 1, 1] - minus_part[:, 0, 0])
    real_part = jnp.concatenate([q_real, u_real], axis=1)
    imag_part = jnp.concatenate([q_imag, u_imag], axis=1)
    return jnp.stack([real_part, imag_part], axis=1).astype(jnp.bfloat16)


def legendre_step(harm_block, table_block):
    cycle_total = table_block.shape[-1]
    evolutions = harm_block.shape[-1] // 4
    contract = (((0,), (0,)), ((), ()))
    plus_part = lax.dot_general(table_block[0], harm_block, contract, preferred_element_type=jnp.float32)
    minus_part = lax.dot_general(table_block[1], harm_block, contract, preferred_element_type=jnp.float32)
    plus_part = plus_part.reshape(cycle_total, 2, 2, evolutions)
    minus_part = minus_part.reshape(cycle_total, 2, 2, evolutions)
    return combine_parts(plus_part, minus_part)


def phase_table(m_values, cell_count, lmax_width):
    pixel_index = jnp.arange(cell_count, dtype=jnp.int32)
    period = 2 * lmax_width
    phase_turns = (m_values[None, :] * pixel_index[:, None]) % period
    angles = phase_turns.astype(jnp.float32) * (2.0 * jnp.pi / period)
    return jnp.stack([jnp.cos(angles), -jnp.sin(angles)], axis=-1).astype(jnp.bfloat16)


def reference(harmonics, legendre, m_values, cycle_cell, phi_cell, offsets):
    spectra = lax.map(lambda paired: legendre_step(paired[0], paired[1]), (harmonics, legendre))
    columns = spectra.shape[-1]
    phase_rows = phase_table(m_values, NPHI, L).astype(jnp.float32)
    cycle_blocks = spectra.reshape(MTOT, R // RD, RD, 2, columns).transpose(1, 0, 2, 3, 4)

    def cycle_block(part):
        summed = jnp.einsum("kmi,mric->rkc", phase_rows, part.astype(jnp.float32), precision=lax.Precision.HIGHEST)
        return (2.0 * summed).astype(jnp.bfloat16)

    field_rows = lax.map(cycle_block, cycle_blocks)
    band_grid = field_rows.reshape(OWNERS, BANDS, RD, NPHI, columns).transpose(1, 0, 2, 3, 4)
    band_grid = band_grid.reshape(BANDS, RB, NPHI, columns)
    padded = jnp.pad(band_grid, ((0, 0), (4, 4), (0, 0), (0, 0)))
    band_of = (jnp.arange(MTOT, dtype=jnp.int32) % BANDS).astype(jnp.int32)
    cycle_blocks_pts = cycle_cell.reshape(MTOT, PD)
    phi_blocks_pts = phi_cell.reshape(MTOT, PD)
    offset_blocks = offsets.reshape(2, MTOT, PD).transpose(1, 2, 0)

    def point_block(packed):
        band_index, cycles_here, phis_here, offsets_here = packed
        band_slab = lax.dynamic_index_in_dim(padded, band_index, 0, keepdims=False)
        tap_index = jnp.arange(8, dtype=jnp.int32)
        row_index = cycles_here[:, None] + 1 + tap_index[None, :]
        col_index = phis_here[:, None] - 3 + tap_index[None, :]
        patches = band_slab[row_index[:, :, None], col_index[:, None, :]]
        weights = tap_weights(offsets_here)
        return jnp.einsum("sab,sabc->sc", weights.astype(jnp.float32), patches.astype(jnp.float32), precision=lax.Precision.HIGHEST)

    lensed = lax.map(point_block, (band_of, cycle_blocks_pts, phi_blocks_pts, offset_blocks))
    return lensed.reshape(PTS, columns)
```

```python
import functools

import jax
import jax.numpy as jnp
from jax import lax
from jax.experimental import pallas as pl
from jax.experimental.pallas import tpu as pltpu
from jax.sharding import PartitionSpec as P

NPHI = 128
LANES = 128
TAPS = 8
MESH = pl.DeviceIdType.MESH
F32 = jnp.float32
BF16 = jnp.bfloat16


def sinc(x):
    t = jnp.pi * x
    small = x == 0.0
    return jnp.where(small, 1.0, jnp.sin(t) / jnp.where(small, 1.0, t))


def taps_of(offset_row):
    steps = lax.broadcasted_iota(jnp.int32, (TAPS, offset_row.shape[1]), 0).astype(F32) - 3.0
    shifts = steps - offset_row
    return sinc(shifts) * sinc(shifts / 4.0)


def kernel(
    dims, harm, leg, m_ref, cell_ref, phi_ref, off_ref, out_ref,
    harm_v, leg_v, acc, pts, phase, weights, send, recv, back, ret,
    load_sems, pts_send, pts_recv, spec_send, spec_recv, ret_send, ret_recv,
):
    owners, bands, depth, period, chunk, prebuilt = dims
    total = owners * bands
    length, columns = harm.shape
    cycles = leg.shape[2]
    evolutions = columns // 4
    width = 2 * evolutions
    rows = cycles // bands
    share = width // owners
    pieces = length // chunk
    pack = LANES // (2 * rows)
    ma = lax.axis_index("ma")
    band = lax.axis_index("band")
    me = ma * bands + band

    def loads(step):
        here = pl.ds(pl.multiple_of(step * chunk, chunk), chunk)
        pairs = [(harm.at[here], harm_v.at[here])]
        for half in range(2):
            pairs.append((leg.at[half, here], leg_v.at[here, pl.ds(half * cycles, cycles)]))
        return [
            pltpu.make_async_copy(src, dst, load_sems.at[n, step])
            for n, (src, dst) in enumerate(pairs)
        ]

    def start_loads(step, carry):
        for copy in loads(step):
            copy.start()
        return carry

    lax.fori_loop(0, pieces, start_loads, 0)

    barrier = pltpu.get_barrier_semaphore()

    def greet(step, carry):
        peer = lax.rem(me + step, total)
        pl.semaphore_signal(
            barrier, inc=1, device_id=(peer // bands, lax.rem(peer, bands)), device_id_type=MESH
        )
        return carry

    lax.fori_loop(1, total, greet, 0)

    pts[ma, 0:TAPS, :] = taps_of(off_ref[0:1, :])
    pts[ma, TAPS:2 * TAPS, :] = taps_of(off_ref[1:2, :])
    row = lax.broadcasted_iota(jnp.int32, (TAPS, LANES), 0)
    pts[ma, 2 * TAPS:3 * TAPS, :] = jnp.where(
        row == 0, cell_ref[...], jnp.where(row == 1, phi_ref[...], 0)
    ).astype(F32)

    pl.semaphore_wait(barrier, total - 1)

    def send_points(step, carry):
        peer = lax.rem(ma + step, owners)
        pltpu.make_async_remote_copy(
            src_ref=pts.at[ma], dst_ref=pts.at[ma], send_sem=pts_send, recv_sem=pts_recv,
            device_id=(peer, band), device_id_type=MESH,
        ).start()
        return carry

    lax.fori_loop(1, owners, send_points, 0)

    eye = lax.broadcasted_iota(jnp.int32, (total, total), 0) == lax.broadcasted_iota(
        jnp.int32, (total, total), 1
    )
    m_column = jnp.sum(jnp.where(eye, m_ref[...].astype(F32), 0.0), axis=1, keepdims=True)
    pixel = lax.broadcasted_iota(jnp.int32, (total, NPHI), 1)
    turns = lax.rem(m_column.astype(jnp.int32) * pixel, period)
    angles = turns.astype(F32) * (2.0 * jnp.pi / period)
    phase[0:total, :] = jnp.cos(angles).astype(BF16)
    phase[total:2 * total, :] = (-jnp.sin(angles)).astype(BF16)

    acc[...] = jnp.zeros_like(acc)

    def multiply(step, carry):
        for copy in loads(step):
            copy.wait()
        here = pl.ds(pl.multiple_of(step * chunk, chunk), chunk)
        acc[...] += lax.dot_general(
            harm_v[here, :], leg_v[here, :], (((0,), (0,)), ((), ())),
            preferred_element_type=F32,
        )
        return carry

    lax.fori_loop(0, pieces, multiply, 0)

    def part(half, which):
        return acc[which * evolutions:(which + 1) * evolutions, half * cycles:(half + 1) * cycles]

    q_real = -(part(0, 0) - part(1, 3))
    q_imag = -(part(0, 1) + part(1, 2))
    u_real = -(part(0, 2) + part(1, 1))
    u_imag = -(part(0, 3) - part(1, 0))
    real = jnp.concatenate([q_real, u_real], axis=0)
    imag = jnp.concatenate([q_imag, u_imag], axis=0)
    spectra = jnp.concatenate([real, imag], axis=1).astype(BF16)

    source = lax.broadcasted_iota(jnp.int32, (2 * cycles, LANES), 0)
    lane = lax.broadcasted_iota(jnp.int32, (2 * cycles, LANES), 1)
    inner = lax.rem(lane, 2 * rows)
    j = lax.rem(inner, rows)
    mine = (lane // (2 * rows)) == lax.rem(me, pack)
    for b in range(bands):
        place = (inner // rows) * cycles + ((j // depth) * bands + b) * depth + lax.rem(j, depth)
        pick = jnp.where(mine & (source == place), 1.0, 0.0).astype(BF16)
        send[b] = jnp.dot(spectra, pick, preferred_element_type=F32).astype(send.dtype)

    def send_spectra(step, carry):
        peer = lax.rem(me + step, total)
        to_ma, to_band = peer // bands, lax.rem(peer, bands)
        pltpu.make_async_remote_copy(
            src_ref=send.at[to_band, pl.ds(pl.multiple_of(to_ma * share, share), share)],
            dst_ref=recv.at[me], send_sem=spec_send, recv_sem=spec_recv,
            device_id=(to_ma, to_band), device_id_type=MESH,
        ).start()
        return carry

    lax.fori_loop(1, total, send_spectra, 0)
    recv[me] = send[band, pl.ds(pl.multiple_of(ma * share, share), share), :]

    others = pl.ds(0, owners - 1)
    pltpu.make_async_copy(pts.at[others], pts.at[others], pts_recv).wait()

    def build(s, column):
        pixels = lax.broadcasted_iota(jnp.int32, (NPHI, LANES), 0)
        ring = lax.broadcasted_iota(jnp.int32, (rows, LANES), 0)
        table = pts[s]
        cell = table[2 * TAPS:2 * TAPS + 1].astype(jnp.int32)
        phi = table[2 * TAPS + 1:2 * TAPS + 2].astype(jnp.int32)
        across = jnp.zeros((rows, LANES), F32)
        beside = jnp.zeros((NPHI, LANES), F32)
        for e in range(TAPS):
            across = jnp.where(ring == cell + (e - 3), table[e:e + 1], across)
            beside = jnp.where(pixels == phi + (e - 3), table[TAPS + e:TAPS + e + 1], beside)
        across = 2.0 * across
        high = beside.astype(BF16)
        low = (beside - high.astype(F32)).astype(BF16)
        mixed = jnp.dot(phase[...], high, preferred_element_type=F32) + jnp.dot(
            phase[...], low, preferred_element_type=F32
        )
        for g in range(total):
            for i in range(2):
                at = (g * 2 + i) * rows
                weights[at:at + rows, column] = (
                    mixed[i * total + g:i * total + g + 1] * across
                ).astype(BF16)

    def build_all(s, carry):
        build(s, pl.ds(pl.multiple_of(s * LANES, LANES), LANES))
        return carry

    if prebuilt:
        lax.fori_loop(0, owners, build_all, 0)

    arrived = pl.ds(0, total - 1)
    pltpu.make_async_copy(recv.at[arrived], recv.at[arrived], spec_recv).wait()
    groups = []
    for h in range(total // pack):
        block = recv[h * pack]
        for extra in range(1, pack):
            block = block + recv[h * pack + extra]
        groups.append(block.astype(BF16))
    lined = jnp.concatenate(groups, axis=1)

    for t in range(owners // 2):
        at = 2 * t * LANES if prebuilt else 0
        if not prebuilt:
            for half in range(2):
                build(2 * t + half, pl.ds(half * LANES, LANES))
        values = jnp.dot(lined, weights[:, at:at + 2 * LANES], preferred_element_type=F32)
        for half in range(2):
            s = 2 * t + half
            back[s] = values[:, half * LANES:(half + 1) * LANES]

            @pl.when(s != ma)
            def _():
                pltpu.make_async_remote_copy(
                    src_ref=back.at[s], dst_ref=ret.at[ma], send_sem=ret_send,
                    recv_sem=ret_recv, device_id=(s, band), device_id_type=MESH,
                ).start()

    ret[ma] = back[ma]
    pltpu.make_async_copy(ret.at[others], ret.at[others], ret_recv).wait()
    out_ref[...] = ret[...].reshape(width, LANES).T

    pltpu.make_async_copy(pts.at[others], pts.at[others], pts_send).wait()
    pltpu.make_async_copy(recv.at[arrived], recv.at[arrived], spec_send).wait()
    pltpu.make_async_copy(back.at[others], back.at[others], ret_send).wait()


def on_device(harmonics, legendre, m_values, cycle_cell, phi_cell, offsets):
    owners, bands = lax.axis_size("ma"), lax.axis_size("band")
    total = owners * bands
    _, length, columns = harmonics.shape
    cycles = legendre.shape[3]
    width = columns // 2
    rows = cycles // bands
    share = width // owners
    points = cycle_cell.shape[0]
    depth = cycles // total
    chunk = min(512, length)
    pieces = length // chunk
    contraction = total * 2 * rows
    prebuilt = contraction * owners * points * 2 <= 16 * 2**20
    kept = owners * points if prebuilt else 2 * points
    wire = BF16 if share % 16 == 0 else F32
    dims = (owners, bands, depth, 2 * length, chunk, prebuilt)
    vmem = pl.BlockSpec(memory_space=pltpu.VMEM)
    anywhere = pl.BlockSpec(memory_space=pl.ANY)
    dma = pltpu.SemaphoreType.DMA
    return pl.pallas_call(
        functools.partial(kernel, dims),
        out_shape=jax.ShapeDtypeStruct((points, width), F32),
        in_specs=[anywhere, anywhere, vmem, vmem, vmem, vmem],
        out_specs=vmem,
        scratch_shapes=[
            pltpu.VMEM((length, columns), BF16),
            pltpu.VMEM((length, 2 * cycles), BF16),
            pltpu.VMEM((columns, 2 * cycles), F32),
            pltpu.VMEM((owners, 3 * TAPS, points), F32),
            pltpu.VMEM((2 * total, NPHI), BF16),
            pltpu.VMEM((contraction, kept), BF16),
            pltpu.VMEM((bands, width, LANES), wire),
            pltpu.VMEM((total, share, LANES), wire),
            pltpu.VMEM((owners, share, points), F32),
            pltpu.VMEM((owners, share, points), F32),
            dma((3, pieces)),
            dma, dma, dma, dma, dma, dma,
        ],
        compiler_params=pltpu.CompilerParams(
            collective_id=0, has_side_effects=True, vmem_limit_bytes=56 * 2**20
        ),
    )(
        harmonics[0], legendre[0], m_values.reshape(1, -1), cycle_cell.reshape(1, -1),
        phi_cell.reshape(1, -1), offsets,
    )


def solution(mesh):
    in_specs = (
        P(("ma", "band"), None, None),
        P(("ma", "band"), None, None, None),
        P(),
        P(("ma", "band")),
        P(("ma", "band")),
        P(None, ("ma", "band")),
    )
    out_specs = P(("ma", "band"), None)
    return jax.shard_map(
        on_device, mesh=mesh, in_specs=in_specs, out_specs=out_specs, check_vma=False
    )
```

```python
import functools

import jax
import jax.numpy as jnp
from jax import lax
from jax.experimental import pallas as pl
from jax.experimental.pallas import tpu as pltpu
from jax.sharding import PartitionSpec as P

NPHI = 128
LANES = 128
TAPS = 8
MESH = pl.DeviceIdType.MESH
F32 = jnp.float32
BF16 = jnp.bfloat16


def quotient(value, by):
    return value >> (by.bit_length() - 1) if by & (by - 1) == 0 else lax.div(value, by)


def remainder(value, by):
    return value & (by - 1) if by & (by - 1) == 0 else lax.rem(value, by)


def sinc(x):
    t = jnp.pi * x
    small = x == 0.0
    return jnp.where(small, 1.0, jnp.sin(t) / jnp.where(small, 1.0, t))


def taps_of(offset_row):
    steps = lax.broadcasted_iota(jnp.int32, (TAPS, offset_row.shape[1]), 0).astype(F32) - 3.0
    shifts = steps - offset_row
    return sinc(shifts) * sinc(shifts / 4.0)


def kernel(
    dims, harm, leg, m_ref, cell_ref, phi_ref, off_ref, out_ref,
    harm_v, leg_v, acc, pts, phase, picks, weights, send, recv, back, ret,
    load_sems, pts_send, pts_recv, spec_send, spec_recv, ret_send, ret_recv,
):
    owners, bands, depth, period, chunk, prebuilt = dims
    total = owners * bands
    length, columns = harm.shape
    cycles = leg.shape[2]
    evolutions = columns // 4
    width = 2 * evolutions
    rows = cycles // bands
    share = width // owners
    pieces = length // chunk
    pack = LANES // (2 * rows)
    ma = lax.axis_index("ma")
    band = lax.axis_index("band")
    me = ma * bands + band
    group = total // 4
    slab = group * 2 * rows
    my_group = quotient(me, group)

    def loads(step):
        here = pl.ds(pl.multiple_of(step * chunk, chunk), chunk)
        pairs = [(harm.at[here], harm_v.at[here])]
        for half in range(2):
            pairs.append((leg.at[half, here], leg_v.at[here, pl.ds(half * cycles, cycles)]))
        return [
            pltpu.make_async_copy(src, dst, load_sems.at[n, step])
            for n, (src, dst) in enumerate(pairs)
        ]

    def start_loads(step, carry):
        for copy in loads(step):
            copy.start()
        return carry

    lax.fori_loop(0, pieces, start_loads, 0)

    barrier = pltpu.get_barrier_semaphore()

    def greet(step, carry):
        peer = remainder(me + step, total)
        pl.semaphore_signal(
            barrier, inc=1, device_id=(quotient(peer, bands), remainder(peer, bands)),
            device_id_type=MESH,
        )
        return carry

    lax.fori_loop(1, total, greet, 0)

    pts[ma, 0:TAPS, :] = taps_of(off_ref[0:1, :])
    pts[ma, TAPS:2 * TAPS, :] = taps_of(off_ref[1:2, :])
    row = lax.broadcasted_iota(jnp.int32, (TAPS, LANES), 0)
    pts[ma, 2 * TAPS:3 * TAPS, :] = jnp.where(
        row == 0, cell_ref[...], jnp.where(row == 1, phi_ref[...], 0)
    ).astype(F32)

    eye = lax.broadcasted_iota(jnp.int32, (total, total), 0) == lax.broadcasted_iota(
        jnp.int32, (total, total), 1
    )
    m_column = jnp.sum(jnp.where(eye, m_ref[...].astype(F32), 0.0), axis=1, keepdims=True)
    pixel = lax.broadcasted_iota(jnp.int32, (total, NPHI), 1)
    turns = remainder(m_column.astype(jnp.int32) * pixel, period)
    angles = turns.astype(F32) * (2.0 * jnp.pi / period)
    phase[0:total, :] = jnp.cos(angles).astype(BF16)
    phase[total:2 * total, :] = (-jnp.sin(angles)).astype(BF16)

    lane = lax.broadcasted_iota(jnp.int32, (1, LANES), 1)
    inner = remainder(lane, 2 * rows)
    j = remainder(inner, rows)
    place = quotient(inner, rows) * cycles + quotient(j, depth) * (bands * depth) + remainder(j, depth)
    place = jnp.where(quotient(lane, 2 * rows) == remainder(me, pack), place, -4 * cycles)
    away = lax.broadcasted_iota(jnp.int32, (2 * cycles, LANES), 0) - place
    for b in range(bands):
        picks[b] = jnp.where(away == b * depth, 1.0, 0.0).astype(BF16)

    acc[...] = jnp.zeros_like(acc)

    def multiply(step, carry):
        for copy in loads(step):
            copy.wait()
        here = pl.ds(pl.multiple_of(step * chunk, chunk), chunk)
        acc[...] += lax.dot_general(
            harm_v[here, :], leg_v[here, :], (((0,), (0,)), ((), ())),
            preferred_element_type=F32,
        )
        return carry

    lax.fori_loop(0, pieces // 2, multiply, 0)

    pl.semaphore_wait(barrier, total - 1)

    def send_points(step, carry):
        peer = remainder(ma + step, owners)
        pltpu.make_async_remote_copy(
            src_ref=pts.at[ma], dst_ref=pts.at[ma], send_sem=pts_send, recv_sem=pts_recv,
            device_id=(peer, band), device_id_type=MESH,
        ).start()
        return carry

    lax.fori_loop(1, owners, send_points, 0)

    lax.fori_loop(pieces // 2, pieces, multiply, 0)

    def part(half, which):
        return acc[which * evolutions:(which + 1) * evolutions, half * cycles:(half + 1) * cycles]

    q_real = -(part(0, 0) - part(1, 3))
    q_imag = -(part(0, 1) + part(1, 2))
    u_real = -(part(0, 2) + part(1, 1))
    u_imag = -(part(0, 3) - part(1, 0))
    real = jnp.concatenate([q_real, u_real], axis=0)
    imag = jnp.concatenate([q_imag, u_imag], axis=0)
    spectra = jnp.concatenate([real, imag], axis=1).astype(BF16)

    for b in range(bands):
        send[b] = jnp.dot(spectra, picks[b], preferred_element_type=F32).astype(send.dtype)

    def send_spectra(step, carry):
        peer = remainder(me + step, total)
        to_ma, to_band = quotient(peer, bands), remainder(peer, bands)
        pltpu.make_async_remote_copy(
            src_ref=send.at[to_band, pl.ds(pl.multiple_of(to_ma * share, share), share)],
            dst_ref=recv.at[me], send_sem=spec_send, recv_sem=spec_recv.at[my_group],
            device_id=(to_ma, to_band), device_id_type=MESH,
        ).start()
        return carry

    lax.fori_loop(1, total, send_spectra, 0)
    recv[me] = send[band, pl.ds(pl.multiple_of(ma * share, share), share), :]

    others = pl.ds(0, owners - 1)
    pltpu.make_async_copy(pts.at[others], pts.at[others], pts_recv).wait()

    def build(s, column):
        pixels = lax.broadcasted_iota(jnp.int32, (NPHI, LANES), 0)
        ring = lax.broadcasted_iota(jnp.int32, (rows, LANES), 0)
        table = pts[s]
        cell = table[2 * TAPS:2 * TAPS + 1].astype(jnp.int32)
        phi = table[2 * TAPS + 1:2 * TAPS + 2].astype(jnp.int32)
        across = jnp.zeros((rows, LANES), F32)
        beside = jnp.zeros((NPHI, LANES), F32)
        for e in range(TAPS):
            across = jnp.where(ring == cell + (e - 3), table[e:e + 1], across)
            beside = jnp.where(pixels == phi + (e - 3), table[TAPS + e:TAPS + e + 1], beside)
        high = beside.astype(BF16)
        low = (beside - high.astype(F32)).astype(BF16)
        mixed = jnp.dot(phase[...], high, preferred_element_type=F32) + jnp.dot(
            phase[...], low, preferred_element_type=F32
        )
        for g in range(total):
            for i in range(2):
                at = (g * 2 + i) * rows
                weights[at:at + rows, column] = (
                    mixed[i * total + g:i * total + g + 1] * across
                ).astype(BF16)

    def build_all(s, carry):
        build(s, pl.ds(pl.multiple_of(s * LANES, LANES), LANES))
        return carry

    if prebuilt:
        lax.fori_loop(0, owners, build_all, 0, unroll=2)

    order = [
        my_group,
        my_group + 1 - 2 * remainder(my_group, 2),
        my_group + 2 - 4 * quotient(my_group, 2),
        3 - my_group,
    ]

    def arrive(n):
        came = pl.ds(0, group - 1 if n == 0 else group)
        pltpu.make_async_copy(recv.at[came], recv.at[came], spec_recv.at[order[n]]).wait()

    def lined(at):
        blocks = []
        for h in range(group // pack):
            block = recv[at * group + h * pack]
            for extra in range(1, pack):
                block = block + recv[at * group + h * pack + extra]
            blocks.append(block.astype(BF16))
        return jnp.concatenate(blocks, axis=1)

    def give(t, values):
        for half in range(2):
            s = 2 * t + half
            back[s] = values[:, half * LANES:(half + 1) * LANES].astype(back.dtype)

            @pl.when(s != ma)
            def _():
                pltpu.make_async_remote_copy(
                    src_ref=back.at[s], dst_ref=ret.at[ma], send_sem=ret_send,
                    recv_sem=ret_recv, device_id=(s, band), device_id_type=MESH,
                ).start()

    if prebuilt:
        sums = [0.0] * (owners // 2)
        for n in range(4):
            arrive(n)
            left = lined(order[n])
            here = pl.ds(pl.multiple_of(order[n] * slab, slab), slab)
            for t in range(owners // 2):
                sums[t] += jnp.dot(
                    left, weights[here, 2 * t * LANES:2 * (t + 1) * LANES],
                    preferred_element_type=F32,
                )
                if n == 3:
                    give(t, sums[t])
    else:
        for n in range(4):
            arrive(n)
        left = jnp.concatenate([lined(n) for n in range(4)], axis=1)
        for t in range(owners // 2):
            for half in range(2):
                build(2 * t + half, pl.ds(half * LANES, LANES))
            give(t, jnp.dot(left, weights[...], preferred_element_type=F32))

    ret[ma] = back[ma]
    pltpu.make_async_copy(ret.at[others], ret.at[others], ret_recv).wait()
    out_ref[...] = ret[...].astype(F32).reshape(width, LANES).T

    pltpu.make_async_copy(pts.at[others], pts.at[others], pts_send).wait()
    arrived = pl.ds(0, total - 1)
    pltpu.make_async_copy(recv.at[arrived], recv.at[arrived], spec_send).wait()
    pltpu.make_async_copy(back.at[others], back.at[others], ret_send).wait()


def on_device(harmonics, legendre, m_values, cycle_cell, phi_cell, offsets):
    owners, bands = lax.axis_size("ma"), lax.axis_size("band")
    total = owners * bands
    _, length, columns = harmonics.shape
    cycles = legendre.shape[3]
    width = columns // 2
    rows = cycles // bands
    share = width // owners
    points = cycle_cell.shape[0]
    depth = cycles // total
    chunk = min(1024, length)
    pieces = length // chunk
    contraction = total * 2 * rows
    prebuilt = contraction * owners * points * 2 <= 16 * 2**20
    kept = owners * points if prebuilt else 2 * points
    wire = BF16 if share % 16 == 0 else F32
    dims = (owners, bands, depth, 2 * length, chunk, prebuilt)
    vmem = pl.BlockSpec(memory_space=pltpu.VMEM)
    anywhere = pl.BlockSpec(memory_space=pl.ANY)
    dma = pltpu.SemaphoreType.DMA
    halved = pl.pallas_call(
        functools.partial(kernel, dims),
        out_shape=jax.ShapeDtypeStruct((points, width), F32),
        in_specs=[anywhere, anywhere, vmem, vmem, vmem, vmem],
        out_specs=vmem,
        scratch_shapes=[
            pltpu.VMEM((length, columns), BF16),
            pltpu.VMEM((length, 2 * cycles), BF16),
            pltpu.VMEM((columns, 2 * cycles), F32),
            pltpu.VMEM((owners, 3 * TAPS, points), F32),
            pltpu.VMEM((2 * total, NPHI), BF16),
            pltpu.VMEM((bands, 2 * cycles, LANES), BF16),
            pltpu.VMEM((contraction, kept), BF16),
            pltpu.VMEM((bands, width, LANES), wire),
            pltpu.VMEM((total, share, LANES), wire),
            pltpu.VMEM((owners, share, points), wire),
            pltpu.VMEM((owners, share, points), wire),
            dma((3, pieces)),
            dma, dma, dma, dma((4,)), dma, dma,
        ],
        compiler_params=pltpu.CompilerParams(
            collective_id=0, has_side_effects=True, vmem_limit_bytes=56 * 2**20
        ),
    )(
        harmonics[0], legendre[0], m_values.reshape(1, -1), cycle_cell.reshape(1, -1),
        phi_cell.reshape(1, -1), offsets,
    )
    return 2.0 * halved


def solution(mesh):
    in_specs = (
        P(("ma", "band"), None, None),
        P(("ma", "band"), None, None, None),
        P(),
        P(("ma", "band")),
        P(("ma", "band")),
        P(None, ("ma", "band")),
    )
    out_specs = P(("ma", "band"), None)
    return jax.shard_map(
        on_device, mesh=mesh, in_specs=in_specs, out_specs=out_specs, check_vma=False
    )
```

```python
import functools

import jax
import jax.numpy as jnp
from jax import lax
from jax.experimental import pallas as pl
from jax.experimental.pallas import tpu as pltpu
from jax.sharding import PartitionSpec as P

NPHI = 128
LANES = 128
TAPS = 8
MESH = pl.DeviceIdType.MESH
F32 = jnp.float32
BF16 = jnp.bfloat16


def quotient(value, by):
    return value >> (by.bit_length() - 1) if by & (by - 1) == 0 else lax.div(value, by)


def remainder(value, by):
    return value & (by - 1) if by & (by - 1) == 0 else lax.rem(value, by)


def sinc(x):
    t = jnp.pi * x
    small = x == 0.0
    return jnp.where(small, 1.0, jnp.sin(t) / jnp.where(small, 1.0, t))


def taps_of(offset_row):
    steps = lax.broadcasted_iota(jnp.int32, (TAPS, offset_row.shape[1]), 0).astype(F32) - 3.0
    shifts = steps - offset_row
    return sinc(shifts) * sinc(shifts / 4.0)


def kernel(
    dims, harm, leg, m_in, cell_in, phi_in, off_in, out_ref,
    harm_v, leg_v, acc, pts, phase, picks, weights, send, recv, back, ret,
    m_ref, cell_ref, phi_ref, off_ref, load_sems, small_sems, pts_send, pts_recv, spec_send, spec_recv, ret_send, ret_recv,
):
    owners, bands, depth, period, chunk, prebuilt = dims
    total = owners * bands
    length, columns = harm.shape
    cycles = leg.shape[2]
    evolutions = columns // 4
    width = 2 * evolutions
    rows = cycles // bands
    share = width // owners
    pieces = length // chunk
    pack = LANES // (2 * rows)
    ma = lax.axis_index("ma")
    band = lax.axis_index("band")
    me = ma * bands + band
    group = total // 4
    slab = group * 2 * rows
    my_group = quotient(me, group)

    def loads(step):
        here = pl.ds(pl.multiple_of(step * chunk, chunk), chunk)
        pairs = [(harm.at[here], harm_v.at[here])]
        for half in range(2):
            pairs.append((leg.at[half, here], leg_v.at[here, pl.ds(half * cycles, cycles)]))
        return [
            pltpu.make_async_copy(src, dst, load_sems.at[n, step])
            for n, (src, dst) in enumerate(pairs)
        ]

    def start_loads(step, carry):
        for copy in loads(step):
            copy.start()
        return carry

    lax.fori_loop(0, 1, start_loads, 0)
    small = [
        pltpu.make_async_copy(src, dst, small_sems.at[n])
        for n, (src, dst) in enumerate(
            [(off_in, off_ref), (cell_in, cell_ref), (phi_in, phi_ref), (m_in, m_ref)]
        )
    ]
    for copy in small:
        copy.start()
    lax.fori_loop(1, pieces, start_loads, 0)

    barrier = pltpu.get_barrier_semaphore()

    def greet(step, carry):
        peer = remainder(me + step, total)
        pl.semaphore_signal(
            barrier, inc=1, device_id=(quotient(peer, bands), remainder(peer, bands)),
            device_id_type=MESH,
        )
        return carry

    lax.fori_loop(1, total, greet, 0)

    for copy in small:
        copy.wait()

    pts[ma, 0:TAPS, :] = taps_of(off_ref[0:1, :])
    pts[ma, TAPS:2 * TAPS, :] = taps_of(off_ref[1:2, :])
    row = lax.broadcasted_iota(jnp.int32, (TAPS, LANES), 0)
    pts[ma, 2 * TAPS:3 * TAPS, :] = jnp.where(
        row == 0, cell_ref[...], jnp.where(row == 1, phi_ref[...], 0)
    ).astype(F32)

    eye = lax.broadcasted_iota(jnp.int32, (total, total), 0) == lax.broadcasted_iota(
        jnp.int32, (total, total), 1
    )
    m_column = jnp.sum(jnp.where(eye, m_ref[...].astype(F32), 0.0), axis=1, keepdims=True)
    pixel = lax.broadcasted_iota(jnp.int32, (total, NPHI), 1)
    turns = remainder(m_column.astype(jnp.int32) * pixel, period)
    angles = turns.astype(F32) * (2.0 * jnp.pi / period)
    phase[0:total, :] = jnp.cos(angles).astype(BF16)
    phase[total:2 * total, :] = (-jnp.sin(angles)).astype(BF16)

    lane = lax.broadcasted_iota(jnp.int32, (1, LANES), 1)
    inner = remainder(lane, 2 * rows)
    j = remainder(inner, rows)
    place = quotient(inner, rows) * cycles + quotient(j, depth) * (bands * depth) + remainder(j, depth)
    place = jnp.where(quotient(lane, 2 * rows) == remainder(me, pack), place, -4 * cycles)
    away = lax.broadcasted_iota(jnp.int32, (2 * cycles, LANES), 0) - place
    for b in range(bands):
        picks[:, b * LANES:(b + 1) * LANES] = jnp.where(away == b * depth, 1.0, 0.0).astype(BF16)

    acc[...] = jnp.zeros_like(acc)

    def multiply(step, carry):
        for copy in loads(step):
            copy.wait()
        here = pl.ds(pl.multiple_of(step * chunk, chunk), chunk)
        acc[...] += lax.dot_general(
            harm_v[here, :], leg_v[here, :], (((0,), (0,)), ((), ())),
            preferred_element_type=F32,
        )
        return carry

    lax.fori_loop(0, pieces // 2, multiply, 0)

    pl.semaphore_wait(barrier, total - 1)

    def send_points(step, carry):
        peer = remainder(ma + step, owners)
        pltpu.make_async_remote_copy(
            src_ref=pts.at[ma], dst_ref=pts.at[ma], send_sem=pts_send, recv_sem=pts_recv,
            device_id=(peer, band), device_id_type=MESH,
        ).start()
        return carry

    lax.fori_loop(1, owners, send_points, 0)

    lax.fori_loop(pieces // 2, pieces, multiply, 0)

    def part(half, which):
        return acc[which * evolutions:(which + 1) * evolutions, half * cycles:(half + 1) * cycles]

    q_real = -(part(0, 0) - part(1, 3))
    q_imag = -(part(0, 1) + part(1, 2))
    u_real = -(part(0, 2) + part(1, 1))
    u_imag = -(part(0, 3) - part(1, 0))
    real = jnp.concatenate([q_real, u_real], axis=0)
    imag = jnp.concatenate([q_imag, u_imag], axis=0)
    spectra = jnp.concatenate([real, imag], axis=1).astype(BF16)

    moved = jnp.dot(spectra, picks[...], preferred_element_type=F32).astype(send.dtype)
    for b in range(bands):
        send[b] = moved[:, b * LANES:(b + 1) * LANES]

    def send_spectra(step, carry):
        peer = remainder(me + step, total)
        to_ma, to_band = quotient(peer, bands), remainder(peer, bands)
        pltpu.make_async_remote_copy(
            src_ref=send.at[to_band, pl.ds(pl.multiple_of(to_ma * share, share), share)],
            dst_ref=recv.at[me], send_sem=spec_send, recv_sem=spec_recv.at[my_group],
            device_id=(to_ma, to_band), device_id_type=MESH,
        ).start()
        return carry

    lax.fori_loop(1, total, send_spectra, 0)
    recv[me] = send[band, pl.ds(pl.multiple_of(ma * share, share), share), :]

    others = pl.ds(0, owners - 1)
    pltpu.make_async_copy(pts.at[others], pts.at[others], pts_recv).wait()

    def build(s, column):
        pixels = lax.broadcasted_iota(jnp.int32, (NPHI, LANES), 0)
        ring = lax.broadcasted_iota(jnp.int32, (rows, LANES), 0)
        table = pts[s]
        cell = table[2 * TAPS:2 * TAPS + 1].astype(jnp.int32)
        phi = table[2 * TAPS + 1:2 * TAPS + 2].astype(jnp.int32)
        across = jnp.zeros((rows, LANES), F32)
        beside = jnp.zeros((NPHI, LANES), F32)
        for e in range(TAPS):
            across = jnp.where(ring == cell + (e - 3), table[e:e + 1], across)
            beside = jnp.where(pixels == phi + (e - 3), table[TAPS + e:TAPS + e + 1], beside)
        high = beside.astype(BF16)
        low = (beside - high.astype(F32)).astype(BF16)
        mixed = jnp.dot(phase[...], high, preferred_element_type=F32) + jnp.dot(
            phase[...], low, preferred_element_type=F32
        )
        for g in range(total):
            for i in range(2):
                at = (g * 2 + i) * rows
                weights[at:at + rows, column] = (
                    mixed[i * total + g:i * total + g + 1] * across
                ).astype(BF16)

    def build_all(s, carry):
        build(s, pl.ds(pl.multiple_of(s * LANES, LANES), LANES))
        return carry

    if prebuilt:
        lax.fori_loop(0, owners, build_all, 0, unroll=2)

    order = [
        my_group,
        my_group + 1 - 2 * remainder(my_group, 2),
        my_group + 2 - 4 * quotient(my_group, 2),
        3 - my_group,
    ]

    def arrive(n):
        came = pl.ds(0, group - 1 if n == 0 else group)
        pltpu.make_async_copy(recv.at[came], recv.at[came], spec_recv.at[order[n]]).wait()

    def lined(at):
        blocks = []
        for h in range(group // pack):
            block = recv[at * group + h * pack]
            for extra in range(1, pack):
                block = block + recv[at * group + h * pack + extra]
            blocks.append(block.astype(BF16))
        return jnp.concatenate(blocks, axis=1)

    def give(t, values):
        for half in range(2):
            s = 2 * t + half
            back[s] = values[:, half * LANES:(half + 1) * LANES].astype(back.dtype)

            @pl.when(s != ma)
            def _():
                pltpu.make_async_remote_copy(
                    src_ref=back.at[s], dst_ref=ret.at[ma], send_sem=ret_send,
                    recv_sem=ret_recv, device_id=(s, band), device_id_type=MESH,
                ).start()

    if prebuilt:
        sums = [0.0] * (owners // 2)
        for n in range(4):
            arrive(n)
            left = lined(order[n])
            here = pl.ds(pl.multiple_of(order[n] * slab, slab), slab)
            for t in range(owners // 2):
                sums[t] += jnp.dot(
                    left, weights[here, 2 * t * LANES:2 * (t + 1) * LANES],
                    preferred_element_type=F32,
                )
                if n == 3:
                    give(t, sums[t])
    else:
        for n in range(4):
            arrive(n)
        left = jnp.concatenate([lined(n) for n in range(4)], axis=1)
        for t in range(owners // 2):
            for half in range(2):
                build(2 * t + half, pl.ds(half * LANES, LANES))
            give(t, jnp.dot(left, weights[...], preferred_element_type=F32))

    ret[ma] = back[ma]
    pltpu.make_async_copy(ret.at[others], ret.at[others], ret_recv).wait()
    out_ref[...] = ret[...].astype(F32).reshape(width, LANES).T

    pltpu.make_async_copy(pts.at[others], pts.at[others], pts_send).wait()
    arrived = pl.ds(0, total - 1)
    pltpu.make_async_copy(recv.at[arrived], recv.at[arrived], spec_send).wait()
    pltpu.make_async_copy(back.at[others], back.at[others], ret_send).wait()


def on_device(harmonics, legendre, m_values, cycle_cell, phi_cell, offsets):
    owners, bands = lax.axis_size("ma"), lax.axis_size("band")
    total = owners * bands
    _, length, columns = harmonics.shape
    cycles = legendre.shape[3]
    width = columns // 2
    rows = cycles // bands
    share = width // owners
    points = cycle_cell.shape[0]
    depth = cycles // total
    chunk = min(1024, length)
    pieces = length // chunk
    contraction = total * 2 * rows
    prebuilt = contraction * owners * points * 2 <= 16 * 2**20
    kept = owners * points if prebuilt else 2 * points
    wire = BF16 if share % 16 == 0 else F32
    dims = (owners, bands, depth, 2 * length, chunk, prebuilt)
    vmem = pl.BlockSpec(memory_space=pltpu.VMEM)
    far = pl.BlockSpec(memory_space=pltpu.HBM)
    dma = pltpu.SemaphoreType.DMA
    halved = pl.pallas_call(
        functools.partial(kernel, dims),
        out_shape=jax.ShapeDtypeStruct((points, width), F32),
        in_specs=[far] * 6,
        out_specs=vmem,
        scratch_shapes=[
            pltpu.VMEM((length, columns), BF16),
            pltpu.VMEM((length, 2 * cycles), BF16),
            pltpu.VMEM((columns, 2 * cycles), F32),
            pltpu.VMEM((owners, 3 * TAPS, points), F32),
            pltpu.VMEM((2 * total, NPHI), BF16),
            pltpu.VMEM((2 * cycles, bands * LANES), BF16),
            pltpu.VMEM((contraction, kept), BF16),
            pltpu.VMEM((bands, width, LANES), wire),
            pltpu.VMEM((total, share, LANES), wire),
            pltpu.VMEM((owners, share, points), wire),
            pltpu.VMEM((owners, share, points), wire),
            pltpu.VMEM((1, total), jnp.int32),
            pltpu.VMEM((1, points), jnp.int32),
            pltpu.VMEM((1, points), jnp.int32),
            pltpu.VMEM((2, points), F32),
            dma((3, pieces)),
            dma((4,)),
            dma, dma, dma, dma((4,)), dma, dma,
        ],
        compiler_params=pltpu.CompilerParams(
            collective_id=0, has_side_effects=True, vmem_limit_bytes=(20 if prebuilt else 56) * 2**20
        ),
    )(
        *[
            pltpu.with_memory_space_constraint(x, pltpu.HBM)
            for x in (
                harmonics[0], legendre[0], m_values.reshape(1, -1), cycle_cell.reshape(1, -1),
                phi_cell.reshape(1, -1), offsets,
            )
        ]
    )
    return 2.0 * halved


def solution(mesh):
    in_specs = (
        P(("ma", "band"), None, None),
        P(("ma", "band"), None, None, None),
        P(),
        P(("ma", "band")),
        P(("ma", "band")),
        P(None, ("ma", "band")),
    )
    out_specs = P(("ma", "band"), None)
    return jax.shard_map(
        on_device, mesh=mesh, in_specs=in_specs, out_specs=out_specs, check_vma=False
    )
```

```python
import functools
import math

import jax
import jax.numpy as jnp
from jax import lax
from jax.experimental import pallas as pl
from jax.experimental.pallas import tpu as pltpu
from jax.sharding import PartitionSpec as P

NPHI = 128
LANES = 128
TAPS = 8
MESH = pl.DeviceIdType.MESH
F32 = jnp.float32
BF16 = jnp.bfloat16


def quotient(value, by):
    return value >> (by.bit_length() - 1) if by & (by - 1) == 0 else lax.div(value, by)


def remainder(value, by):
    return value & (by - 1) if by & (by - 1) == 0 else lax.rem(value, by)


def short_sine(y):
    square = y * y
    series = 0.0
    for n in (13, 11, 9, 7, 5, 3):
        series = (series + (-1.0) ** (n // 2) / math.factorial(n)) * square
    return y + y * series


def turn_sine(turn, period):
    turn = jnp.where(turn > period // 2, turn - period, turn)
    turn = jnp.where(turn > period // 4, period // 2 - turn, turn)
    turn = jnp.where(turn < -(period // 4), -(period // 2) - turn, turn)
    return short_sine(turn.astype(F32) * (2.0 * math.pi / period))


def taps_of(offset_row):
    tap = lax.broadcasted_iota(jnp.int32, (TAPS, offset_row.shape[1]), 0)
    shifts = tap.astype(F32) - 3.0 - offset_row
    whole = short_sine(math.pi * jnp.minimum(offset_row, 1.0 - offset_row))
    whole = jnp.where(remainder(tap, 2) == 1, -whole, whole)
    quarter = shifts / 4.0
    mirrored = jnp.where(quarter > 0.5, 1.0 - quarter, quarter)
    mirrored = jnp.where(quarter < -0.5, -1.0 - quarter, mirrored)
    wide = short_sine(math.pi * mirrored)
    zero = shifts == 0.0
    safe = jnp.where(zero, 1.0, shifts) * math.pi
    return jnp.where(zero, 1.0, (whole / safe) * (wide / (safe / 4.0)))


def kernel(
    dims, harm, leg, m_in, cell_in, phi_in, off_in, out_ref,
    harm_v, leg_v, acc, pts, phase, picks, weights, send, recv, back, ret,
    m_ref, cell_ref, phi_ref, off_ref, load_sems, small_sems, pts_send, pts_recv, spec_send, spec_recv, ret_send, ret_recv,
):
    owners, bands, depth, period, chunk, prebuilt = dims
    total = owners * bands
    length, columns = harm.shape
    cycles = leg.shape[2]
    evolutions = columns // 4
    width = 2 * evolutions
    rows = cycles // bands
    share = width // owners
    pieces = length // chunk
    pack = LANES // (2 * rows)
    lines = share // pack
    ma = lax.axis_index("ma")
    band = lax.axis_index("band")
    me = ma * bands + band
    group = total // 4
    slab = group * 2 * rows
    my_group = quotient(me, group)

    def loads(step):
        here = pl.ds(step * chunk if isinstance(step, int) else pl.multiple_of(step * chunk, chunk), chunk)
        pairs = [(harm.at[here], harm_v.at[here])]
        for half in range(2):
            pairs.append((leg.at[half, here], leg_v.at[here, pl.ds(half * cycles, cycles)]))
        return [
            pltpu.make_async_copy(src, dst, load_sems.at[n, step])
            for n, (src, dst) in enumerate(pairs)
        ]

    def start_loads(step, carry):
        for copy in loads(step):
            copy.start()
        return carry

    lax.fori_loop(0, 1, start_loads, 0)
    small = [
        pltpu.make_async_copy(src, dst, small_sems.at[n])
        for n, (src, dst) in enumerate(
            [(off_in, off_ref), (cell_in, cell_ref), (phi_in, phi_ref), (m_in, m_ref)]
        )
    ]
    for copy in small:
        copy.start()
    lax.fori_loop(1, pieces, start_loads, 0)

    barrier = pltpu.get_barrier_semaphore()

    def greet(step, carry):
        peer = remainder(me + step, total)
        pl.semaphore_signal(
            barrier, inc=1, device_id=(quotient(peer, bands), remainder(peer, bands)),
            device_id_type=MESH,
        )
        return carry

    lax.fori_loop(1, total, greet, 0)

    for copy in small:
        copy.wait()

    pts[ma, 0:TAPS, :] = taps_of(off_ref[0:1, :])
    pts[ma, TAPS:2 * TAPS, :] = taps_of(off_ref[1:2, :])
    row = lax.broadcasted_iota(jnp.int32, (TAPS, LANES), 0)
    pts[ma, 2 * TAPS:3 * TAPS, :] = jnp.where(
        row == 0, cell_ref[...], jnp.where(row == 1, phi_ref[...], 0)
    ).astype(F32)

    eye = lax.broadcasted_iota(jnp.int32, (total, total), 0) == lax.broadcasted_iota(
        jnp.int32, (total, total), 1
    )
    m_column = jnp.sum(jnp.where(eye, m_ref[...].astype(F32), 0.0), axis=1, keepdims=True)
    pixel = lax.broadcasted_iota(jnp.int32, (total, NPHI), 1)
    turns = remainder(m_column.astype(jnp.int32) * pixel, period)
    quarter_on = remainder(turns + period // 4, period)
    phase[0:total, :] = turn_sine(quarter_on, period).astype(BF16)
    phase[total:2 * total, :] = (-turn_sine(turns, period)).astype(BF16)

    lane = lax.broadcasted_iota(jnp.int32, (1, LANES), 1)
    inner = remainder(lane, 2 * rows)
    j = remainder(inner, rows)
    place = quotient(inner, rows) * cycles + quotient(j, depth) * (bands * depth) + remainder(j, depth)
    away = lax.broadcasted_iota(jnp.int32, (2 * cycles, LANES), 0) - place
    for b in range(bands):
        picks[:, b * LANES:(b + 1) * LANES] = jnp.where(away == b * depth, 1.0, 0.0).astype(BF16)

    acc[...] = jnp.zeros_like(acc)

    def multiply(step, carry):
        for copy in loads(step):
            copy.wait()
        here = pl.ds(step * chunk, chunk)
        acc[...] += lax.dot_general(
            harm_v[here, :], leg_v[here, :], (((0,), (0,)), ((), ())),
            preferred_element_type=F32,
        )
        return carry

    for step in range(pieces // 2):
        multiply(step, 0)

    pl.semaphore_wait(barrier, total - 1)

    def send_points(step, carry):
        peer = remainder(ma + step, owners)
        pltpu.make_async_remote_copy(
            src_ref=pts.at[ma], dst_ref=pts.at[ma], send_sem=pts_send, recv_sem=pts_recv,
            device_id=(peer, band), device_id_type=MESH,
        ).start()
        return carry

    lax.fori_loop(1, owners, send_points, 0)

    for step in range(pieces // 2, pieces):
        multiply(step, 0)

    def part(half, which):
        return acc[which * evolutions:(which + 1) * evolutions, half * cycles:(half + 1) * cycles]

    q_real = -(part(0, 0) - part(1, 3))
    q_imag = -(part(0, 1) + part(1, 2))
    u_real = -(part(0, 2) + part(1, 1))
    u_imag = -(part(0, 3) - part(1, 0))
    real = jnp.concatenate([q_real, u_real], axis=0)
    imag = jnp.concatenate([q_imag, u_imag], axis=0)
    spectra = jnp.concatenate([real, imag], axis=1).astype(BF16)

    moved = jnp.dot(spectra, picks[...], preferred_element_type=F32)
    first = quotient(lane, 2 * rows) == remainder(me, pack)
    for b in range(bands):
        band_part = moved[:, b * LANES:(b + 1) * LANES]
        for q in range(owners):
            block = band_part[q * share:q * share + lines]
            if pack == 2:
                block = jnp.where(first, block, band_part[q * share + lines:(q + 1) * share])
            send[b, q] = block.astype(BF16)

    def send_spectra(step, carry):
        peer = remainder(me + step, total)
        to_ma, to_band = quotient(peer, bands), remainder(peer, bands)
        pltpu.make_async_remote_copy(
            src_ref=send.at[to_band, to_ma],
            dst_ref=recv.at[me], send_sem=spec_send, recv_sem=spec_recv.at[my_group],
            device_id=(to_ma, to_band), device_id_type=MESH,
        ).start()
        return carry

    lax.fori_loop(1, total, send_spectra, 0)
    recv[me] = send[band, ma]

    others = pl.ds(0, owners - 1)
    pltpu.make_async_copy(pts.at[others], pts.at[others], pts_recv).wait()

    def build(s, column):
        pixels = lax.broadcasted_iota(jnp.int32, (NPHI, LANES), 0)
        ring = lax.broadcasted_iota(jnp.int32, (rows, LANES), 0)
        table = pts[s]
        cell = table[2 * TAPS:2 * TAPS + 1].astype(jnp.int32)
        phi = table[2 * TAPS + 1:2 * TAPS + 2].astype(jnp.int32)
        across = jnp.zeros((rows, LANES), F32)
        beside = jnp.zeros((NPHI, LANES), F32)
        for e in range(TAPS):
            across = jnp.where(ring == cell + (e - 3), table[e:e + 1], across)
            beside = jnp.where(pixels == phi + (e - 3), table[TAPS + e:TAPS + e + 1], beside)
        high = beside.astype(BF16)
        low = (beside - high.astype(F32)).astype(BF16)
        mixed = jnp.dot(phase[...], high, preferred_element_type=F32) + jnp.dot(
            phase[...], low, preferred_element_type=F32
        )
        for g in range(total):
            for i in range(2):
                at = (g * 2 + i) * rows
                weights[at:at + rows, column] = (
                    mixed[i * total + g:i * total + g + 1] * across
                ).astype(BF16)

    def build_all(s, carry):
        build(s, pl.ds(pl.multiple_of(s * LANES, LANES), LANES))
        return carry

    if prebuilt:
        lax.fori_loop(0, owners, build_all, 0, unroll=2)

    order = [
        my_group,
        my_group + 1 - 2 * remainder(my_group, 2),
        my_group + 2 - 4 * quotient(my_group, 2),
        3 - my_group,
    ]

    def arrive(n):
        came = pl.ds(0, group - 1 if n == 0 else group)
        pltpu.make_async_copy(recv.at[came], recv.at[came], spec_recv.at[order[n]]).wait()

    low_half = lax.broadcasted_iota(jnp.int32, (lines, LANES), 1) < LANES // 2

    def lined(at):
        blocks = []
        for h in range(group // pack):
            block = recv[at * group + h * pack].astype(F32)
            if pack == 2:
                other = recv[at * group + h * pack + 1].astype(F32)
                upper = jnp.where(low_half, other, block)
                block = jnp.concatenate(
                    [jnp.where(low_half, block, other), pltpu.roll(upper, LANES // 2, 1)], axis=0
                )
            blocks.append(block.astype(BF16))
        return jnp.concatenate(blocks, axis=1)

    def give(t, values):
        for half in range(2):
            s = 2 * t + half
            back[s] = values[:, half * LANES:(half + 1) * LANES].astype(back.dtype)

            @pl.when(s != ma)
            def _():
                pltpu.make_async_remote_copy(
                    src_ref=back.at[s], dst_ref=ret.at[ma], send_sem=ret_send,
                    recv_sem=ret_recv, device_id=(s, band), device_id_type=MESH,
                ).start()

    if prebuilt:
        sums = [0.0] * (owners // 2)
        for n in range(4):
            arrive(n)
            left = lined(order[n])
            here = pl.ds(pl.multiple_of(order[n] * slab, slab), slab)
            for t in range(owners // 2):
                sums[t] += jnp.dot(
                    left, weights[here, 2 * t * LANES:2 * (t + 1) * LANES],
                    preferred_element_type=F32,
                )
                if n == 3:
                    give(t, sums[t])
    else:
        for n in range(4):
            arrive(n)
        left = jnp.concatenate([lined(n) for n in range(4)], axis=1)
        for t in range(owners // 2):
            for half in range(2):
                build(2 * t + half, pl.ds(half * LANES, LANES))
            give(t, jnp.dot(left, weights[...], preferred_element_type=F32))

    ret[ma] = back[ma]
    pltpu.make_async_copy(ret.at[others], ret.at[others], ret_recv).wait()
    out_ref[...] = ret[...].astype(F32).reshape(width, LANES).T

    pltpu.make_async_copy(pts.at[others], pts.at[others], pts_send).wait()
    arrived = pl.ds(0, total - 1)
    pltpu.make_async_copy(recv.at[arrived], recv.at[arrived], spec_send).wait()
    pltpu.make_async_copy(back.at[others], back.at[others], ret_send).wait()


def on_device(harmonics, legendre, m_values, cycle_cell, phi_cell, offsets):
    owners, bands = lax.axis_size("ma"), lax.axis_size("band")
    total = owners * bands
    _, length, columns = harmonics.shape
    cycles = legendre.shape[3]
    width = columns // 2
    rows = cycles // bands
    share = width // owners
    points = cycle_cell.shape[0]
    depth = cycles // total
    pack = LANES // (2 * rows)
    chunk = min(1024, length)
    pieces = length // chunk
    contraction = total * 2 * rows
    prebuilt = contraction * owners * points * 2 <= 16 * 2**20
    kept = owners * points if prebuilt else 2 * points
    wire = BF16 if share % 16 == 0 else F32
    dims = (owners, bands, depth, 2 * length, chunk, prebuilt)
    vmem = pl.BlockSpec(memory_space=pltpu.VMEM)
    far = pl.BlockSpec(memory_space=pltpu.HBM)
    dma = pltpu.SemaphoreType.DMA
    halved = pl.pallas_call(
        functools.partial(kernel, dims),
        out_shape=jax.ShapeDtypeStruct((points, width), F32),
        in_specs=[far] * 6,
        out_specs=vmem,
        scratch_shapes=[
            pltpu.VMEM((length, columns), BF16),
            pltpu.VMEM((length, 2 * cycles), BF16),
            pltpu.VMEM((columns, 2 * cycles), F32),
            pltpu.VMEM((owners, 3 * TAPS, points), F32),
            pltpu.VMEM((2 * total, NPHI), BF16),
            pltpu.VMEM((2 * cycles, bands * LANES), BF16),
            pltpu.VMEM((contraction, kept), BF16),
            pltpu.VMEM((bands, owners, share // pack, LANES), BF16),
            pltpu.VMEM((total, share // pack, LANES), BF16),
            pltpu.VMEM((owners, share, points), wire),
            pltpu.VMEM((owners, share, points), wire),
            pltpu.VMEM((1, total), jnp.int32),
            pltpu.VMEM((1, points), jnp.int32),
            pltpu.VMEM((1, points), jnp.int32),
            pltpu.VMEM((2, points), F32),
            dma((3, pieces)),
            dma((4,)),
            dma, dma, dma, dma((4,)), dma, dma,
        ],
        compiler_params=pltpu.CompilerParams(
            collective_id=0, has_side_effects=True, vmem_limit_bytes=(20 if prebuilt else 56) * 2**20
        ),
    )(
        *[
            pltpu.with_memory_space_constraint(x, pltpu.HBM)
            for x in (
                harmonics[0], legendre[0], m_values.reshape(1, -1), cycle_cell.reshape(1, -1),
                phi_cell.reshape(1, -1), offsets,
            )
        ]
    )
    return 2.0 * halved


def solution(mesh):
    in_specs = (
        P(("ma", "band"), None, None),
        P(("ma", "band"), None, None, None),
        P(),
        P(("ma", "band")),
        P(("ma", "band")),
        P(None, ("ma", "band")),
    )
    out_specs = P(("ma", "band"), None)
    return jax.shard_map(
        on_device, mesh=mesh, in_specs=in_specs, out_specs=out_specs, check_vma=False
    )
```

```python
import functools
import math

import jax
import jax.numpy as jnp
from jax import lax
from jax.experimental import pallas as pl
from jax.experimental.pallas import tpu as pltpu
from jax.sharding import PartitionSpec as P

NPHI = 128
LANES = 128
TAPS = 8
MESH = pl.DeviceIdType.MESH
F32 = jnp.float32
BF16 = jnp.bfloat16


def quotient(value, by):
    return value >> (by.bit_length() - 1) if by & (by - 1) == 0 else lax.div(value, by)


def remainder(value, by):
    return value & (by - 1) if by & (by - 1) == 0 else lax.rem(value, by)


def short_sine(y):
    square = y * y
    series = 0.0
    for n in (13, 11, 9, 7, 5, 3):
        series = (series + (-1.0) ** (n // 2) / math.factorial(n)) * square
    return y + y * series


def turn_sine(turn, period):
    turn = jnp.where(turn > period // 2, turn - period, turn)
    turn = jnp.where(turn > period // 4, period // 2 - turn, turn)
    turn = jnp.where(turn < -(period // 4), -(period // 2) - turn, turn)
    return short_sine(turn.astype(F32) * (2.0 * math.pi / period))


def taps_of(offset_row):
    tap = lax.broadcasted_iota(jnp.int32, (TAPS, offset_row.shape[1]), 0)
    shifts = tap.astype(F32) - 3.0 - offset_row
    whole = short_sine(math.pi * jnp.minimum(offset_row, 1.0 - offset_row))
    whole = jnp.where(remainder(tap, 2) == 1, -whole, whole)
    quarter = shifts / 4.0
    mirrored = jnp.where(quarter > 0.5, 1.0 - quarter, quarter)
    mirrored = jnp.where(quarter < -0.5, -1.0 - quarter, mirrored)
    wide = short_sine(math.pi * mirrored)
    zero = shifts == 0.0
    safe = jnp.where(zero, 1.0, shifts) * math.pi
    return jnp.where(zero, 1.0, (whole / safe) * (wide / (safe / 4.0)))


def kernel(
    dims, harm, leg, m_in, cell_in, phi_in, off_in, out_ref,
    harm_v, leg_v, acc, pts, phase, picks, acrosses, besides, mixed, weights, send, recv, back, ret,
    m_ref, cell_ref, phi_ref, off_ref, load_sems, small_sems, pts_send, pts_recv, spec_send, spec_recv, ret_send, ret_recv,
):
    owners, bands, depth, period, chunk, prebuilt = dims
    total = owners * bands
    length, columns = harm.shape
    cycles = leg.shape[2]
    evolutions = columns // 4
    width = 2 * evolutions
    rows = cycles // bands
    share = width // owners
    pieces = length // chunk
    pack = LANES // (2 * rows)
    lines = share // pack
    ma = lax.axis_index("ma")
    band = lax.axis_index("band")
    me = ma * bands + band
    group = total // 4
    slab = group * 2 * rows
    my_group = quotient(me, group)
    order = [
        my_group,
        my_group + 1 - 2 * remainder(my_group, 2),
        my_group + 2 - 4 * quotient(my_group, 2),
        3 - my_group,
    ]

    def loads(step):
        here = pl.ds(step * chunk if isinstance(step, int) else pl.multiple_of(step * chunk, chunk), chunk)
        pairs = [(harm.at[here], harm_v.at[here])]
        for half in range(2):
            pairs.append((leg.at[half, here], leg_v.at[here, pl.ds(half * cycles, cycles)]))
        return [
            pltpu.make_async_copy(src, dst, load_sems.at[n, step])
            for n, (src, dst) in enumerate(pairs)
        ]

    def start_loads(step, carry):
        for copy in loads(step):
            copy.start()
        return carry

    lax.fori_loop(0, 1, start_loads, 0)
    small = [
        pltpu.make_async_copy(src, dst, small_sems.at[n])
        for n, (src, dst) in enumerate(
            [(off_in, off_ref), (cell_in, cell_ref), (phi_in, phi_ref), (m_in, m_ref)]
        )
    ]
    for copy in small:
        copy.start()
    lax.fori_loop(1, pieces, start_loads, 0)

    barrier = pltpu.get_barrier_semaphore()

    def greet(step, carry):
        peer = remainder(me + step, total)
        pl.semaphore_signal(
            barrier, inc=1, device_id=(quotient(peer, bands), remainder(peer, bands)),
            device_id_type=MESH,
        )
        return carry

    lax.fori_loop(1, total, greet, 0)

    for copy in small:
        copy.wait()

    pts[ma, 0:TAPS, :] = taps_of(off_ref[0:1, :])
    pts[ma, TAPS:2 * TAPS, :] = taps_of(off_ref[1:2, :])
    row = lax.broadcasted_iota(jnp.int32, (TAPS, LANES), 0)
    pts[ma, 2 * TAPS:3 * TAPS, :] = jnp.where(
        row == 0, cell_ref[...], jnp.where(row == 1, phi_ref[...], 0)
    ).astype(F32)

    eye = lax.broadcasted_iota(jnp.int32, (total, total), 0) == lax.broadcasted_iota(
        jnp.int32, (total, total), 1
    )
    m_column = jnp.sum(jnp.where(eye, m_ref[...].astype(F32), 0.0), axis=1, keepdims=True)
    pixel = lax.broadcasted_iota(jnp.int32, (total, NPHI), 1)
    turns = remainder(m_column.astype(jnp.int32) * pixel, period)
    quarter_on = remainder(turns + period // 4, period)
    phase[0:total, :] = turn_sine(quarter_on, period).astype(BF16)
    phase[total:2 * total, :] = (-turn_sine(turns, period)).astype(BF16)

    lane = lax.broadcasted_iota(jnp.int32, (1, LANES), 1)
    inner = remainder(lane, 2 * rows)
    j = remainder(inner, rows)
    place = quotient(inner, rows) * cycles + quotient(j, depth) * (bands * depth) + remainder(j, depth)
    away = lax.broadcasted_iota(jnp.int32, (2 * cycles, LANES), 0) - place
    for b in range(bands):
        picks[:, b * LANES:(b + 1) * LANES] = jnp.where(away == b * depth, 1.0, 0.0).astype(BF16)

    acc[...] = jnp.zeros_like(acc)

    def multiply(step, carry):
        for copy in loads(step):
            copy.wait()
        here = pl.ds(step * chunk, chunk)
        acc[...] += lax.dot_general(
            harm_v[here, :], leg_v[here, :], (((0,), (0,)), ((), ())),
            preferred_element_type=F32,
        )
        return carry

    for step in range(pieces // 4):
        multiply(step, 0)

    pl.semaphore_wait(barrier, total - 1)

    def send_points(step, carry):
        peer = remainder(ma + step, owners)
        pltpu.make_async_remote_copy(
            src_ref=pts.at[ma], dst_ref=pts.at[ma], send_sem=pts_send, recv_sem=pts_recv,
            device_id=(peer, band), device_id_type=MESH,
        ).start()
        return carry

    lax.fori_loop(1, owners, send_points, 0)

    for step in range(pieces // 4, pieces):
        multiply(step, 0)

    def part(half, which):
        return acc[which * evolutions:(which + 1) * evolutions, half * cycles:(half + 1) * cycles]

    q_real = -(part(0, 0) - part(1, 3))
    q_imag = -(part(0, 1) + part(1, 2))
    u_real = -(part(0, 2) + part(1, 1))
    u_imag = -(part(0, 3) - part(1, 0))
    real = jnp.concatenate([q_real, u_real], axis=0)
    imag = jnp.concatenate([q_imag, u_imag], axis=0)
    spectra = jnp.concatenate([real, imag], axis=1).astype(BF16)

    moved = jnp.dot(spectra, picks[...], preferred_element_type=F32)
    first = quotient(lane, 2 * rows) == remainder(me, pack)
    for b in range(bands):
        band_part = moved[:, b * LANES:(b + 1) * LANES]
        for q in range(owners):
            block = band_part[q * share:q * share + lines]
            if pack == 2:
                block = jnp.where(first, block, band_part[q * share + lines:(q + 1) * share])
            send[b, q] = block.astype(BF16)

    for n in (3, 2, 1, 0):
        def send_spectra(step, carry):
            peer = order[n] * group + remainder(me + step, group)
            to_ma, to_band = quotient(peer, bands), remainder(peer, bands)
            pltpu.make_async_remote_copy(
                src_ref=send.at[to_band, to_ma], dst_ref=recv.at[me], send_sem=spec_send,
                recv_sem=spec_recv.at[my_group], device_id=(to_ma, to_band),
                device_id_type=MESH,
            ).start()
            return carry

        lax.fori_loop(1 if n == 0 else 0, group, send_spectra, 0)
    recv[me] = send[band, ma]

    others = pl.ds(0, owners - 1)
    pltpu.make_async_copy(pts.at[others], pts.at[others], pts_recv).wait()

    def spread(s, column):
        pixels = lax.broadcasted_iota(jnp.int32, (NPHI, LANES), 0)
        ring = lax.broadcasted_iota(jnp.int32, (rows, LANES), 0)
        table = pts[s]
        cell = table[2 * TAPS:2 * TAPS + 1].astype(jnp.int32)
        phi = table[2 * TAPS + 1:2 * TAPS + 2].astype(jnp.int32)
        across = jnp.zeros((rows, LANES), F32)
        beside = jnp.zeros((NPHI, LANES), F32)
        for e in range(TAPS):
            across = jnp.where(ring == cell + (e - 3), table[e:e + 1], across)
            beside = jnp.where(pixels == phi + (e - 3), table[TAPS + e:TAPS + e + 1], beside)
        high = beside.astype(BF16)
        acrosses[:, column] = across
        besides[0:NPHI, column] = high
        besides[NPHI:2 * NPHI, column] = (beside - high.astype(F32)).astype(BF16)

    def mix():
        mixed[...] = jnp.dot(
            jnp.concatenate([phase[...], phase[...]], axis=1), besides[...],
            preferred_element_type=F32,
        )

    def build(column):
        across = acrosses[:, column]
        factors = mixed[:, column]
        for g in range(total):
            for i in range(2):
                at = (g * 2 + i) * rows
                weights[at:at + rows, column] = (
                    factors[i * total + g:i * total + g + 1] * across
                ).astype(BF16)

    def block_of(s):
        return pl.ds(pl.multiple_of(s * LANES, LANES), LANES)

    def spread_one(s, carry):
        spread(s, block_of(s))
        return carry

    def build_one(s, carry):
        build(block_of(s))
        return carry

    if prebuilt:
        lax.fori_loop(0, owners, spread_one, 0, unroll=4)
        mix()
        lax.fori_loop(0, owners, build_one, 0, unroll=2)

    def arrive(n):
        came = pl.ds(0, group - 1 if n == 0 else group)
        pltpu.make_async_copy(recv.at[came], recv.at[came], spec_recv.at[order[n]]).wait()

    low_half = lax.broadcasted_iota(jnp.int32, (lines, LANES), 1) < LANES // 2

    def lined(at):
        blocks = []
        for h in range(group // pack):
            block = recv[at * group + h * pack].astype(F32)
            if pack == 2:
                other = recv[at * group + h * pack + 1].astype(F32)
                upper = jnp.where(low_half, other, block)
                block = jnp.concatenate(
                    [jnp.where(low_half, block, other), pltpu.roll(upper, LANES // 2, 1)], axis=0
                )
            blocks.append(block.astype(BF16))
        return jnp.concatenate(blocks, axis=1)

    def give(t, values):
        for half in range(2):
            s = 2 * t + half
            back[s] = values[:, half * LANES:(half + 1) * LANES].astype(back.dtype)

            @pl.when(s != ma)
            def _():
                pltpu.make_async_remote_copy(
                    src_ref=back.at[s], dst_ref=ret.at[ma], send_sem=ret_send,
                    recv_sem=ret_recv, device_id=(s, band), device_id_type=MESH,
                ).start()

    if prebuilt:
        pairs = order[::-1] if owners == 8 else list(range(owners // 2))
        sums = [0.0] * len(pairs)
        for n in range(4):
            arrive(n)
            left = lined(order[n])
            here = pl.ds(pl.multiple_of(order[n] * slab, slab), slab)
            for k, t in enumerate(pairs):
                both = pl.ds(pl.multiple_of(t * (2 * LANES), 2 * LANES), 2 * LANES)
                sums[k] += jnp.dot(left, weights[here, both], preferred_element_type=F32)
                if n == 3:
                    give(t, sums[k])
    else:
        for n in range(4):
            arrive(n)
        left = jnp.concatenate([lined(n) for n in range(4)], axis=1)
        for t in range(owners // 2):
            for half in range(2):
                spread(2 * t + half, pl.ds(half * LANES, LANES))
            mix()
            for half in range(2):
                build(pl.ds(half * LANES, LANES))
            give(t, jnp.dot(left, weights[...], preferred_element_type=F32))

    ret[ma] = back[ma]
    pltpu.make_async_copy(ret.at[others], ret.at[others], ret_recv).wait()
    out_ref[...] = ret[...].astype(F32).reshape(width, LANES).T

    pltpu.make_async_copy(pts.at[others], pts.at[others], pts_send).wait()
    arrived = pl.ds(0, total - 1)
    pltpu.make_async_copy(recv.at[arrived], recv.at[arrived], spec_send).wait()
    pltpu.make_async_copy(back.at[others], back.at[others], ret_send).wait()


def on_device(harmonics, legendre, m_values, cycle_cell, phi_cell, offsets):
    owners, bands = lax.axis_size("ma"), lax.axis_size("band")
    total = owners * bands
    _, length, columns = harmonics.shape
    cycles = legendre.shape[3]
    width = columns // 2
    rows = cycles // bands
    share = width // owners
    points = cycle_cell.shape[0]
    depth = cycles // total
    pack = LANES // (2 * rows)
    chunk = min(1024, length)
    pieces = length // chunk
    contraction = total * 2 * rows
    prebuilt = contraction * owners * points * 2 <= 16 * 2**20
    kept = owners * points if prebuilt else 2 * points
    wire = BF16 if share % 16 == 0 else F32
    dims = (owners, bands, depth, 2 * length, chunk, prebuilt)
    vmem = pl.BlockSpec(memory_space=pltpu.VMEM)
    far = pl.BlockSpec(memory_space=pltpu.HBM)
    dma = pltpu.SemaphoreType.DMA
    halved = pl.pallas_call(
        functools.partial(kernel, dims),
        out_shape=jax.ShapeDtypeStruct((points, width), F32),
        in_specs=[far] * 6,
        out_specs=vmem,
        scratch_shapes=[
            pltpu.VMEM((length, columns), BF16),
            pltpu.VMEM((length, 2 * cycles), BF16),
            pltpu.VMEM((columns, 2 * cycles), F32),
            pltpu.VMEM((owners, 3 * TAPS, points), F32),
            pltpu.VMEM((2 * total, NPHI), BF16),
            pltpu.VMEM((2 * cycles, bands * LANES), BF16),
            pltpu.VMEM((rows, kept), F32),
            pltpu.VMEM((2 * NPHI, kept), BF16),
            pltpu.VMEM((2 * total, kept), F32),
            pltpu.VMEM((contraction, kept), BF16),
            pltpu.VMEM((bands, owners, share // pack, LANES), BF16),
            pltpu.VMEM((total, share // pack, LANES), BF16),
            pltpu.VMEM((owners, share, points), wire),
            pltpu.VMEM((owners, share, points), wire),
            pltpu.VMEM((1, total), jnp.int32),
            pltpu.VMEM((1, points), jnp.int32),
            pltpu.VMEM((1, points), jnp.int32),
            pltpu.VMEM((2, points), F32),
            dma((3, pieces)),
            dma((4,)),
            dma, dma, dma, dma((4,)), dma, dma,
        ],
        compiler_params=pltpu.CompilerParams(
            collective_id=0, has_side_effects=True, vmem_limit_bytes=(20 if prebuilt else 56) * 2**20
        ),
    )(
        *[
            pltpu.with_memory_space_constraint(x, pltpu.HBM)
            for x in (
                harmonics[0], legendre[0], m_values.reshape(1, -1), cycle_cell.reshape(1, -1),
                phi_cell.reshape(1, -1), offsets,
            )
        ]
    )
    return 2.0 * halved


def solution(mesh):
    in_specs = (
        P(("ma", "band"), None, None),
        P(("ma", "band"), None, None, None),
        P(),
        P(("ma", "band")),
        P(("ma", "band")),
        P(None, ("ma", "band")),
    )
    out_specs = P(("ma", "band"), None)
    return jax.shard_map(
        on_device, mesh=mesh, in_specs=in_specs, out_specs=out_specs, check_vma=False
    )
```

```python
import functools
import math

import jax
import jax.numpy as jnp
from jax import lax
from jax.experimental import pallas as pl
from jax.experimental.pallas import tpu as pltpu
from jax.sharding import PartitionSpec as P

NPHI = 128
LANES = 128
TAPS = 8
MESH = pl.DeviceIdType.MESH
F32 = jnp.float32
BF16 = jnp.bfloat16


def quotient(value, by):
    return value >> (by.bit_length() - 1) if by & (by - 1) == 0 else lax.div(value, by)


def remainder(value, by):
    return value & (by - 1) if by & (by - 1) == 0 else lax.rem(value, by)


def repeat(begin, end, body):
    if end - begin <= 32:
        for step in range(begin, end):
            body(step, 0)
    else:
        lax.fori_loop(begin, end, body, 0)


def short_sine(y):
    square = y * y
    series = 0.0
    for n in (13, 11, 9, 7, 5, 3):
        series = (series + (-1.0) ** (n // 2) / math.factorial(n)) * square
    return y + y * series


def turn_sine(turn, period):
    turn = jnp.where(turn > period // 2, turn - period, turn)
    turn = jnp.where(turn > period // 4, period // 2 - turn, turn)
    turn = jnp.where(turn < -(period // 4), -(period // 2) - turn, turn)
    return short_sine(turn.astype(F32) * (2.0 * math.pi / period))


def taps_of(offset_row):
    tap = lax.broadcasted_iota(jnp.int32, (TAPS, offset_row.shape[1]), 0)
    shifts = tap.astype(F32) - 3.0 - offset_row
    whole = short_sine(math.pi * jnp.minimum(offset_row, 1.0 - offset_row))
    whole = jnp.where(remainder(tap, 2) == 1, -whole, whole)
    quarter = shifts / 4.0
    mirrored = jnp.where(quarter > 0.5, 1.0 - quarter, quarter)
    mirrored = jnp.where(quarter < -0.5, -1.0 - quarter, mirrored)
    wide = short_sine(math.pi * mirrored)
    zero = shifts == 0.0
    safe = jnp.where(zero, 1.0, shifts) * math.pi
    return jnp.where(zero, 1.0, (whole / safe) * (wide / (safe / 4.0)))


def kernel(
    dims, harm, leg, m_in, cell_in, phi_in, off_in, out_ref,
    harm_v, leg_v, acc, pts, phase, picks, acrosses, besides, mixed, weights, send, recv, back, ret,
    m_ref, cell_ref, phi_ref, off_ref, load_sems, small_sems, pts_send, pts_recv, spec_send, spec_recv, ret_send, ret_recv,
):
    owners, bands, depth, period, chunk, prebuilt = dims
    total = owners * bands
    length, columns = harm.shape
    cycles = leg.shape[2]
    evolutions = columns // 4
    width = 2 * evolutions
    rows = cycles // bands
    share = width // owners
    pieces = length // chunk
    pack = LANES // (2 * rows)
    lines = share // pack
    ma = lax.axis_index("ma")
    band = lax.axis_index("band")
    me = ma * bands + band
    group = total // 4
    slab = group * 2 * rows
    my_group = quotient(me, group)
    order = [
        my_group,
        my_group + 1 - 2 * remainder(my_group, 2),
        my_group + 2 - 4 * quotient(my_group, 2),
        3 - my_group,
    ]

    def loads(step):
        here = pl.ds(step * chunk if isinstance(step, int) else pl.multiple_of(step * chunk, chunk), chunk)
        pairs = [(harm.at[here], harm_v.at[here])]
        for half in range(2):
            pairs.append((leg.at[half, here], leg_v.at[here, pl.ds(half * cycles, cycles)]))
        return [
            pltpu.make_async_copy(src, dst, load_sems.at[n, step])
            for n, (src, dst) in enumerate(pairs)
        ]

    def start_loads(step, carry):
        for copy in loads(step):
            copy.start()
        return carry

    repeat(0, 1, start_loads)
    small = [
        pltpu.make_async_copy(src, dst, small_sems.at[n])
        for n, (src, dst) in enumerate(
            [(off_in, off_ref), (cell_in, cell_ref), (phi_in, phi_ref), (m_in, m_ref)]
        )
    ]
    for copy in small:
        copy.start()
    repeat(1, pieces, start_loads)

    barrier = pltpu.get_barrier_semaphore()

    def greet(step, carry):
        peer = remainder(me + step, total)
        pl.semaphore_signal(
            barrier, inc=1, device_id=(quotient(peer, bands), remainder(peer, bands)),
            device_id_type=MESH,
        )
        return carry

    repeat(1, total, greet)

    for copy in small:
        copy.wait()

    pts[ma, 0:TAPS, :] = taps_of(off_ref[0:1, :])
    pts[ma, TAPS:2 * TAPS, :] = taps_of(off_ref[1:2, :])
    row = lax.broadcasted_iota(jnp.int32, (TAPS, LANES), 0)
    pts[ma, 2 * TAPS:3 * TAPS, :] = jnp.where(
        row == 0, cell_ref[...], jnp.where(row == 1, phi_ref[...], 0)
    ).astype(F32)

    eye = lax.broadcasted_iota(jnp.int32, (total, total), 0) == lax.broadcasted_iota(
        jnp.int32, (total, total), 1
    )
    m_column = jnp.sum(jnp.where(eye, m_ref[...].astype(F32), 0.0), axis=1, keepdims=True)
    pixel = lax.broadcasted_iota(jnp.int32, (total, NPHI), 1)
    turns = remainder(m_column.astype(jnp.int32) * pixel, period)
    quarter_on = remainder(turns + period // 4, period)
    phase[0:total, :] = turn_sine(quarter_on, period).astype(BF16)
    phase[total:2 * total, :] = (-turn_sine(turns, period)).astype(BF16)

    lane = lax.broadcasted_iota(jnp.int32, (1, LANES), 1)
    inner = remainder(lane, 2 * rows)
    j = remainder(inner, rows)
    place = quotient(inner, rows) * cycles + quotient(j, depth) * (bands * depth) + remainder(j, depth)
    away = lax.broadcasted_iota(jnp.int32, (2 * cycles, LANES), 0) - place
    for b in range(bands):
        picks[:, b * LANES:(b + 1) * LANES] = jnp.where(away == b * depth, 1.0, 0.0).astype(BF16)

    acc[...] = jnp.zeros_like(acc)

    def multiply(step, carry):
        for copy in loads(step):
            copy.wait()
        here = pl.ds(step * chunk, chunk)
        acc[...] += lax.dot_general(
            harm_v[here, :], leg_v[here, :], (((0,), (0,)), ((), ())),
            preferred_element_type=F32,
        )
        return carry

    for step in range(pieces // 2):
        multiply(step, 0)

    pl.semaphore_wait(barrier, total - 1)

    def send_points(step, carry):
        peer = remainder(ma + step, owners)
        pltpu.make_async_remote_copy(
            src_ref=pts.at[ma], dst_ref=pts.at[ma], send_sem=pts_send, recv_sem=pts_recv,
            device_id=(peer, band), device_id_type=MESH,
        ).start()
        return carry

    repeat(1, owners, send_points)

    for step in range(pieces // 2, pieces):
        multiply(step, 0)

    def part(half, which):
        return acc[which * evolutions:(which + 1) * evolutions, half * cycles:(half + 1) * cycles]

    q_real = -(part(0, 0) - part(1, 3))
    q_imag = -(part(0, 1) + part(1, 2))
    u_real = -(part(0, 2) + part(1, 1))
    u_imag = -(part(0, 3) - part(1, 0))
    real = jnp.concatenate([q_real, u_real], axis=0)
    imag = jnp.concatenate([q_imag, u_imag], axis=0)
    spectra = jnp.concatenate([real, imag], axis=1).astype(BF16)

    moved = jnp.dot(spectra, picks[...], preferred_element_type=F32)
    first = quotient(lane, 2 * rows) == remainder(me, pack)
    for b in range(bands):
        band_part = moved[:, b * LANES:(b + 1) * LANES]
        for q in range(owners):
            block = band_part[q * share:q * share + lines]
            if pack == 2:
                block = jnp.where(first, block, band_part[q * share + lines:(q + 1) * share])
            send[b, q] = block.astype(BF16)

    for n in (3, 2, 1, 0):
        def send_spectra(step, carry):
            peer = order[n] * group + remainder(me + step, group)
            to_ma, to_band = quotient(peer, bands), remainder(peer, bands)
            pltpu.make_async_remote_copy(
                src_ref=send.at[to_band, to_ma], dst_ref=recv.at[me], send_sem=spec_send,
                recv_sem=spec_recv.at[my_group], device_id=(to_ma, to_band),
                device_id_type=MESH,
            ).start()
            return carry

        repeat(1 if n == 0 else 0, group, send_spectra)
    recv[me] = send[band, ma]

    others = pl.ds(0, owners - 1)
    pltpu.make_async_copy(pts.at[others], pts.at[others], pts_recv).wait()

    def spread(s, column):
        pixels = lax.broadcasted_iota(jnp.int32, (NPHI, LANES), 0)
        ring = lax.broadcasted_iota(jnp.int32, (rows, LANES), 0)
        table = pts[s]
        cell = table[2 * TAPS:2 * TAPS + 1].astype(jnp.int32)
        phi = table[2 * TAPS + 1:2 * TAPS + 2].astype(jnp.int32)
        across = jnp.zeros((rows, LANES), F32)
        beside = jnp.zeros((NPHI, LANES), F32)
        for e in range(TAPS):
            across = jnp.where(ring == cell + (e - 3), table[e:e + 1], across)
            beside = jnp.where(pixels == phi + (e - 3), table[TAPS + e:TAPS + e + 1], beside)
        high = beside.astype(BF16)
        acrosses[:, column] = across
        besides[0:NPHI, column] = high
        besides[NPHI:2 * NPHI, column] = (beside - high.astype(F32)).astype(BF16)

    def mix():
        mixed[...] = jnp.dot(
            jnp.concatenate([phase[...], phase[...]], axis=1), besides[...],
            preferred_element_type=F32,
        )

    def build(column):
        across = acrosses[:, column]
        factors = mixed[:, column]
        for g in range(total):
            for i in range(2):
                at = (g * 2 + i) * rows
                weights[at:at + rows, column] = (
                    factors[i * total + g:i * total + g + 1] * across
                ).astype(BF16)

    def block_of(s):
        return pl.ds(pl.multiple_of(s * LANES, LANES), LANES)

    def spread_one(s, carry):
        spread(s, block_of(s))
        return carry

    def build_one(s, carry):
        build(block_of(s))
        return carry

    if prebuilt:
        lax.fori_loop(0, owners, spread_one, 0, unroll=4)
        mix()
        lax.fori_loop(0, owners, build_one, 0, unroll=2)

    def arrive(n):
        came = pl.ds(0, group - 1 if n == 0 else group)
        pltpu.make_async_copy(recv.at[came], recv.at[came], spec_recv.at[order[n]]).wait()

    low_half = lax.broadcasted_iota(jnp.int32, (lines, LANES), 1) < LANES // 2

    def lined(at):
        blocks = []
        for h in range(group // pack):
            block = recv[at * group + h * pack].astype(F32)
            if pack == 2:
                other = recv[at * group + h * pack + 1].astype(F32)
                upper = jnp.where(low_half, other, block)
                block = jnp.concatenate(
                    [jnp.where(low_half, block, other), pltpu.roll(upper, LANES // 2, 1)], axis=0
                )
            blocks.append(block.astype(BF16))
        return jnp.concatenate(blocks, axis=1)

    def give(t, values):
        for half in range(2):
            s = 2 * t + half
            back[s] = values[:, half * LANES:(half + 1) * LANES].astype(back.dtype)

            @pl.when(s != ma)
            def _():
                pltpu.make_async_remote_copy(
                    src_ref=back.at[s], dst_ref=ret.at[ma], send_sem=ret_send,
                    recv_sem=ret_recv, device_id=(s, band), device_id_type=MESH,
                ).start()

    if prebuilt:
        pairs = order[::-1] if owners == 8 else list(range(owners // 2))
        sums = [0.0] * len(pairs)
        for n in range(4):
            arrive(n)
            left = lined(order[n])
            here = pl.ds(pl.multiple_of(order[n] * slab, slab), slab)
            for k, t in enumerate(pairs):
                both = pl.ds(pl.multiple_of(t * (2 * LANES), 2 * LANES), 2 * LANES)
                sums[k] += jnp.dot(left, weights[here, both], preferred_element_type=F32)
                if n == 3:
                    give(t, sums[k])
    else:
        for n in range(4):
            arrive(n)
        left = jnp.concatenate([lined(n) for n in range(4)], axis=1)
        for t in range(owners // 2):
            for half in range(2):
                spread(2 * t + half, pl.ds(half * LANES, LANES))
            mix()
            for half in range(2):
                build(pl.ds(half * LANES, LANES))
            give(t, jnp.dot(left, weights[...], preferred_element_type=F32))

    ret[ma] = back[ma]
    pltpu.make_async_copy(ret.at[others], ret.at[others], ret_recv).wait()
    out_ref[...] = ret[...].astype(F32).reshape(width, LANES).T

    pltpu.make_async_copy(pts.at[others], pts.at[others], pts_send).wait()
    arrived = pl.ds(0, total - 1)
    pltpu.make_async_copy(recv.at[arrived], recv.at[arrived], spec_send).wait()
    pltpu.make_async_copy(back.at[others], back.at[others], ret_send).wait()


def on_device(harmonics, legendre, m_values, cycle_cell, phi_cell, offsets):
    owners, bands = lax.axis_size("ma"), lax.axis_size("band")
    total = owners * bands
    _, length, columns = harmonics.shape
    cycles = legendre.shape[3]
    width = columns // 2
    rows = cycles // bands
    share = width // owners
    points = cycle_cell.shape[0]
    depth = cycles // total
    pack = LANES // (2 * rows)
    chunk = min(1024, length)
    pieces = length // chunk
    contraction = total * 2 * rows
    prebuilt = contraction * owners * points * 2 <= 16 * 2**20
    kept = owners * points if prebuilt else 2 * points
    wire = BF16 if share % 16 == 0 else F32
    dims = (owners, bands, depth, 2 * length, chunk, prebuilt)
    vmem = pl.BlockSpec(memory_space=pltpu.VMEM)
    far = pl.BlockSpec(memory_space=pltpu.HBM)
    dma = pltpu.SemaphoreType.DMA
    halved = pl.pallas_call(
        functools.partial(kernel, dims),
        out_shape=jax.ShapeDtypeStruct((points, width), F32),
        in_specs=[far] * 6,
        out_specs=vmem,
        scratch_shapes=[
            pltpu.VMEM((length, columns), BF16),
            pltpu.VMEM((length, 2 * cycles), BF16),
            pltpu.VMEM((columns, 2 * cycles), F32),
            pltpu.VMEM((owners, 3 * TAPS, points), F32),
            pltpu.VMEM((2 * total, NPHI), BF16),
            pltpu.VMEM((2 * cycles, bands * LANES), BF16),
            pltpu.VMEM((rows, kept), F32),
            pltpu.VMEM((2 * NPHI, kept), BF16),
            pltpu.VMEM((2 * total, kept), F32),
            pltpu.VMEM((contraction, kept), BF16),
            pltpu.VMEM((bands, owners, share // pack, LANES), BF16),
            pltpu.VMEM((total, share // pack, LANES), BF16),
            pltpu.VMEM((owners, share, points), wire),
            pltpu.VMEM((owners, share, points), wire),
            pltpu.VMEM((1, total), jnp.int32),
            pltpu.VMEM((1, points), jnp.int32),
            pltpu.VMEM((1, points), jnp.int32),
            pltpu.VMEM((2, points), F32),
            dma((3, pieces)),
            dma((4,)),
            dma, dma, dma, dma((4,)), dma, dma,
        ],
        compiler_params=pltpu.CompilerParams(
            collective_id=0, has_side_effects=True, vmem_limit_bytes=(20 if prebuilt else 56) * 2**20
        ),
    )(
        *[
            pltpu.with_memory_space_constraint(x, pltpu.HBM)
            for x in (
                harmonics[0], legendre[0], m_values.reshape(1, -1), cycle_cell.reshape(1, -1),
                phi_cell.reshape(1, -1), offsets,
            )
        ]
    )
    return 2.0 * halved


def solution(mesh):
    in_specs = (
        P(("ma", "band"), None, None),
        P(("ma", "band"), None, None, None),
        P(),
        P(("ma", "band")),
        P(("ma", "band")),
        P(None, ("ma", "band")),
    )
    out_specs = P(("ma", "band"), None)
    return jax.shard_map(
        on_device, mesh=mesh, in_specs=in_specs, out_specs=out_specs, check_vma=False
    )
```

```python
import functools
import math

import jax
import jax.numpy as jnp
from jax import lax
from jax.experimental import pallas as pl
from jax.experimental.pallas import tpu as pltpu
from jax.sharding import PartitionSpec as P

NPHI = 128
LANES = 128
TAPS = 8
MESH = pl.DeviceIdType.MESH
F32 = jnp.float32
BF16 = jnp.bfloat16


def quotient(value, by):
    return value >> (by.bit_length() - 1) if by & (by - 1) == 0 else lax.div(value, by)


def remainder(value, by):
    return value & (by - 1) if by & (by - 1) == 0 else lax.rem(value, by)


def short_sine(y):
    square = y * y
    series = 0.0
    for n in (13, 11, 9, 7, 5, 3):
        series = (series + (-1.0) ** (n // 2) / math.factorial(n)) * square
    return y + y * series


def turn_sine(turn, period):
    turn = jnp.where(turn > period // 2, turn - period, turn)
    turn = jnp.where(turn > period // 4, period // 2 - turn, turn)
    turn = jnp.where(turn < -(period // 4), -(period // 2) - turn, turn)
    return short_sine(turn.astype(F32) * (2.0 * math.pi / period))


def taps_of(offset_row):
    tap = lax.broadcasted_iota(jnp.int32, (TAPS, offset_row.shape[1]), 0)
    shifts = tap.astype(F32) - 3.0 - offset_row
    whole = short_sine(math.pi * jnp.minimum(offset_row, 1.0 - offset_row))
    whole = jnp.where(remainder(tap, 2) == 1, -whole, whole)
    quarter = shifts / 4.0
    mirrored = jnp.where(quarter > 0.5, 1.0 - quarter, quarter)
    mirrored = jnp.where(quarter < -0.5, -1.0 - quarter, mirrored)
    wide = short_sine(math.pi * mirrored)
    zero = shifts == 0.0
    safe = jnp.where(zero, 1.0, shifts) * math.pi
    return jnp.where(zero, 1.0, (whole / safe) * (wide / (safe / 4.0)))


def kernel(
    dims, harm, leg, m_in, cell_in, phi_in, off_in, out_ref,
    harm_v, leg_v, acc, pts, phase, picks, weights, send, recv, back, ret,
    m_ref, cell_ref, phi_ref, off_ref, load_sems, small_sems, pts_send, pts_recv, spec_send, spec_recv, ret_send, ret_recv,
):
    owners, bands, depth, period, chunk, prebuilt = dims
    total = owners * bands
    length, columns = harm.shape
    cycles = leg.shape[2]
    evolutions = columns // 4
    width = 2 * evolutions
    rows = cycles // bands
    share = width // owners
    pieces = length // chunk
    pack = LANES // (2 * rows)
    lines = share // pack
    ma = lax.axis_index("ma")
    band = lax.axis_index("band")
    me = ma * bands + band
    group = total // 4
    slab = group * 2 * rows
    my_group = quotient(me, group)

    def loads(step):
        here = pl.ds(step * chunk if isinstance(step, int) else pl.multiple_of(step * chunk, chunk), chunk)
        pairs = [(harm.at[here], harm_v.at[here])]
        for half in range(2):
            pairs.append((leg.at[half, here], leg_v.at[here, pl.ds(half * cycles, cycles)]))
        return [
            pltpu.make_async_copy(src, dst, load_sems.at[n, step])
            for n, (src, dst) in enumerate(pairs)
        ]

    def start_loads(step, carry):
        for copy in loads(step):
            copy.start()
        return carry

    lax.fori_loop(0, 1, start_loads, 0)
    small = [
        pltpu.make_async_copy(src, dst, small_sems.at[n])
        for n, (src, dst) in enumerate(
            [(off_in, off_ref), (cell_in, cell_ref), (phi_in, phi_ref), (m_in, m_ref)]
        )
    ]
    for copy in small:
        copy.start()
    lax.fori_loop(1, pieces, start_loads, 0)

    barrier = pltpu.get_barrier_semaphore()

    def greet(step, carry):
        peer = remainder(me + step, total)
        pl.semaphore_signal(
            barrier, inc=1, device_id=(quotient(peer, bands), remainder(peer, bands)),
            device_id_type=MESH,
        )
        return carry

    lax.fori_loop(1, total, greet, 0)

    for copy in small:
        copy.wait()

    pts[ma, 0:TAPS, :] = taps_of(off_ref[0:1, :])
    pts[ma, TAPS:2 * TAPS, :] = taps_of(off_ref[1:2, :])
    row = lax.broadcasted_iota(jnp.int32, (TAPS, LANES), 0)
    pts[ma, 2 * TAPS:3 * TAPS, :] = jnp.where(
        row == 0, cell_ref[...], jnp.where(row == 1, phi_ref[...], 0)
    ).astype(F32)

    eye = lax.broadcasted_iota(jnp.int32, (total, total), 0) == lax.broadcasted_iota(
        jnp.int32, (total, total), 1
    )
    m_column = jnp.sum(jnp.where(eye, m_ref[...].astype(F32), 0.0), axis=1, keepdims=True)
    pixel = lax.broadcasted_iota(jnp.int32, (total, NPHI), 1)
    turns = remainder(m_column.astype(jnp.int32) * pixel, period)
    quarter_on = remainder(turns + period // 4, period)
    phase[0:total, :] = turn_sine(quarter_on, period).astype(BF16)
    phase[total:2 * total, :] = (-turn_sine(turns, period)).astype(BF16)

    lane = lax.broadcasted_iota(jnp.int32, (1, LANES), 1)
    inner = remainder(lane, 2 * rows)
    j = remainder(inner, rows)
    place = quotient(inner, rows) * cycles + quotient(j, depth) * (bands * depth) + remainder(j, depth)
    away = lax.broadcasted_iota(jnp.int32, (2 * cycles, LANES), 0) - place
    for b in range(bands):
        picks[:, b * LANES:(b + 1) * LANES] = jnp.where(away == b * depth, 1.0, 0.0).astype(BF16)

    acc[...] = jnp.zeros_like(acc)

    def multiply(step, carry):
        for copy in loads(step):
            copy.wait()
        here = pl.ds(pl.multiple_of(step * chunk, chunk), chunk)
        acc[...] += lax.dot_general(
            harm_v[here, :], leg_v[here, :], (((0,), (0,)), ((), ())),
            preferred_element_type=F32,
        )
        return carry

    lax.fori_loop(0, pieces // 2, multiply, 0)

    pl.semaphore_wait(barrier, total - 1)

    def send_points(step, carry):
        peer = remainder(ma + step, owners)
        pltpu.make_async_remote_copy(
            src_ref=pts.at[ma], dst_ref=pts.at[ma], send_sem=pts_send, recv_sem=pts_recv,
            device_id=(peer, band), device_id_type=MESH,
        ).start()
        return carry

    lax.fori_loop(1, owners, send_points, 0)

    lax.fori_loop(pieces // 2, pieces, multiply, 0)

    def part(half, which):
        return acc[which * evolutions:(which + 1) * evolutions, half * cycles:(half + 1) * cycles]

    q_real = -(part(0, 0) - part(1, 3))
    q_imag = -(part(0, 1) + part(1, 2))
    u_real = -(part(0, 2) + part(1, 1))
    u_imag = -(part(0, 3) - part(1, 0))
    real = jnp.concatenate([q_real, u_real], axis=0)
    imag = jnp.concatenate([q_imag, u_imag], axis=0)
    spectra = jnp.concatenate([real, imag], axis=1).astype(BF16)

    moved = jnp.dot(spectra, picks[...], preferred_element_type=F32)
    first = quotient(lane, 2 * rows) == remainder(me, pack)
    for b in range(bands):
        band_part = moved[:, b * LANES:(b + 1) * LANES]
        for q in range(owners):
            block = band_part[q * share:q * share + lines]
            if pack == 2:
                block = jnp.where(first, block, band_part[q * share + lines:(q + 1) * share])
            send[b, q] = block.astype(BF16)

    def send_spectra(step, carry):
        peer = remainder(me + step, total)
        to_ma, to_band = quotient(peer, bands), remainder(peer, bands)
        pltpu.make_async_remote_copy(
            src_ref=send.at[to_band, to_ma],
            dst_ref=recv.at[me], send_sem=spec_send, recv_sem=spec_recv.at[my_group],
            device_id=(to_ma, to_band), device_id_type=MESH,
        ).start()
        return carry

    lax.fori_loop(1, total, send_spectra, 0)
    recv[me] = send[band, ma]

    others = pl.ds(0, owners - 1)
    pltpu.make_async_copy(pts.at[others], pts.at[others], pts_recv).wait()

    def build(s, column):
        pixels = lax.broadcasted_iota(jnp.int32, (NPHI, LANES), 0)
        ring = lax.broadcasted_iota(jnp.int32, (rows, LANES), 0)
        table = pts[s]
        cell = table[2 * TAPS:2 * TAPS + 1].astype(jnp.int32)
        phi = table[2 * TAPS + 1:2 * TAPS + 2].astype(jnp.int32)
        across = jnp.zeros((rows, LANES), F32)
        beside = jnp.zeros((NPHI, LANES), F32)
        for e in range(TAPS):
            across = jnp.where(ring == cell + (e - 3), table[e:e + 1], across)
            beside = jnp.where(pixels == phi + (e - 3), table[TAPS + e:TAPS + e + 1], beside)
        high = beside.astype(BF16)
        low = (beside - high.astype(F32)).astype(BF16)
        mixed = jnp.dot(phase[...], high, preferred_element_type=F32) + jnp.dot(
            phase[...], low, preferred_element_type=F32
        )
        for g in range(total):
            for i in range(2):
                at = (g * 2 + i) * rows
                weights[at:at + rows, column] = (
                    mixed[i * total + g:i * total + g + 1] * across
                ).astype(BF16)

    def build_all(s, carry):
        build(s, pl.ds(pl.multiple_of(s * LANES, LANES), LANES))
        return carry

    if prebuilt:
        lax.fori_loop(0, owners, build_all, 0)

    order = [
        my_group,
        my_group + 1 - 2 * remainder(my_group, 2),
        my_group + 2 - 4 * quotient(my_group, 2),
        3 - my_group,
    ]

    def arrive(n):
        came = pl.ds(0, group - 1 if n == 0 else group)
        pltpu.make_async_copy(recv.at[came], recv.at[came], spec_recv.at[order[n]]).wait()

    low_half = lax.broadcasted_iota(jnp.int32, (lines, LANES), 1) < LANES // 2

    def lined(at):
        blocks = []
        for h in range(group // pack):
            block = recv[at * group + h * pack].astype(F32)
            if pack == 2:
                other = recv[at * group + h * pack + 1].astype(F32)
                upper = jnp.where(low_half, other, block)
                block = jnp.concatenate(
                    [jnp.where(low_half, block, other), pltpu.roll(upper, LANES // 2, 1)], axis=0
                )
            blocks.append(block.astype(BF16))
        return jnp.concatenate(blocks, axis=1)

    def give(t, values):
        for half in range(2):
            s = 2 * t + half
            back[s] = values[:, half * LANES:(half + 1) * LANES].astype(back.dtype)

            @pl.when(s != ma)
            def _():
                pltpu.make_async_remote_copy(
                    src_ref=back.at[s], dst_ref=ret.at[ma], send_sem=ret_send,
                    recv_sem=ret_recv, device_id=(s, band), device_id_type=MESH,
                ).start()

    if prebuilt:
        sums = [0.0] * (owners // 2)
        for n in range(4):
            arrive(n)
            left = lined(order[n])
            here = pl.ds(pl.multiple_of(order[n] * slab, slab), slab)
            for t in range(owners // 2):
                sums[t] += jnp.dot(
                    left, weights[here, 2 * t * LANES:2 * (t + 1) * LANES],
                    preferred_element_type=F32,
                )
                if n == 3:
                    give(t, sums[t])
    else:
        for n in range(4):
            arrive(n)
        left = jnp.concatenate([lined(n) for n in range(4)], axis=1)
        for t in range(owners // 2):
            for half in range(2):
                build(2 * t + half, pl.ds(half * LANES, LANES))
            give(t, jnp.dot(left, weights[...], preferred_element_type=F32))

    ret[ma] = back[ma]
    pltpu.make_async_copy(ret.at[others], ret.at[others], ret_recv).wait()
    out_ref[...] = ret[...].astype(F32).reshape(width, LANES).T

    pltpu.make_async_copy(pts.at[others], pts.at[others], pts_send).wait()
    arrived = pl.ds(0, total - 1)
    pltpu.make_async_copy(recv.at[arrived], recv.at[arrived], spec_send).wait()
    pltpu.make_async_copy(back.at[others], back.at[others], ret_send).wait()


def on_device(harmonics, legendre, m_values, cycle_cell, phi_cell, offsets):
    owners, bands = lax.axis_size("ma"), lax.axis_size("band")
    total = owners * bands
    _, length, columns = harmonics.shape
    cycles = legendre.shape[3]
    width = columns // 2
    rows = cycles // bands
    share = width // owners
    points = cycle_cell.shape[0]
    depth = cycles // total
    pack = LANES // (2 * rows)
    chunk = min(1024, length)
    pieces = length // chunk
    contraction = total * 2 * rows
    prebuilt = contraction * owners * points * 2 <= 16 * 2**20
    kept = owners * points if prebuilt else 2 * points
    wire = BF16 if share % 16 == 0 else F32
    dims = (owners, bands, depth, 2 * length, chunk, prebuilt)
    vmem = pl.BlockSpec(memory_space=pltpu.VMEM)
    far = pl.BlockSpec(memory_space=pltpu.HBM)
    dma = pltpu.SemaphoreType.DMA
    halved = pl.pallas_call(
        functools.partial(kernel, dims),
        out_shape=jax.ShapeDtypeStruct((points, width), F32),
        in_specs=[far] * 6,
        out_specs=vmem,
        scratch_shapes=[
            pltpu.VMEM((length, columns), BF16),
            pltpu.VMEM((length, 2 * cycles), BF16),
            pltpu.VMEM((columns, 2 * cycles), F32),
            pltpu.VMEM((owners, 3 * TAPS, points), F32),
            pltpu.VMEM((2 * total, NPHI), BF16),
            pltpu.VMEM((2 * cycles, bands * LANES), BF16),
            pltpu.VMEM((contraction, kept), BF16),
            pltpu.VMEM((bands, owners, share // pack, LANES), BF16),
            pltpu.VMEM((total, share // pack, LANES), BF16),
            pltpu.VMEM((owners, share, points), wire),
            pltpu.VMEM((owners, share, points), wire),
            pltpu.VMEM((1, total), jnp.int32),
            pltpu.VMEM((1, points), jnp.int32),
            pltpu.VMEM((1, points), jnp.int32),
            pltpu.VMEM((2, points), F32),
            dma((3, pieces)),
            dma((4,)),
            dma, dma, dma, dma((4,)), dma, dma,
        ],
        compiler_params=pltpu.CompilerParams(
            collective_id=0, has_side_effects=True, vmem_limit_bytes=(20 if prebuilt else 56) * 2**20
        ),
    )(
        *[
            pltpu.with_memory_space_constraint(x, pltpu.HBM)
            for x in (
                harmonics[0], legendre[0], m_values.reshape(1, -1), cycle_cell.reshape(1, -1),
                phi_cell.reshape(1, -1), offsets,
            )
        ]
    )
    return 2.0 * halved


def solution(mesh):
    in_specs = (
        P(("ma", "band"), None, None),
        P(("ma", "band"), None, None, None),
        P(),
        P(("ma", "band")),
        P(("ma", "band")),
        P(None, ("ma", "band")),
    )
    out_specs = P(("ma", "band"), None)
    return jax.shard_map(
        on_device, mesh=mesh, in_specs=in_specs, out_specs=out_specs, check_vma=False
    )
```
